32 devices in a mesh: rep: 2 (over y), node: 4 (over x, core), local: 4 (over z).
Axes of the slice: x: 2, y: 2, z: 4, core: 2. Of those that a mesh axis runs over, the one named last changes fastest.
Arguments:
- grad_out: bfloat16 [1024, 3584], P(('rep', 'node', 'local')), parts along dimension 0, may hold values from -6 to 6
- routes: int32 [1024, 8], P(('rep', 'node', 'local')), parts along dimension 0, may hold values from 0 to 15, as said below
- combine: bfloat16 [1024, 8], P(('rep', 'node', 'local')), parts along dimension 0, may hold values from 0.049804688 to 1
- hidden_cache: bfloat16 [32, 256, 1024], P(('rep', 'node', 'local')), parts along dimension 0, may hold values from -0.1875 to 0.1875
- down_weight: bfloat16 [16, 1024, 3584], P(('node', 'local')), may hold values from -0.09375 to 0.09375
Outputs:
- d_hidden: bfloat16 [32, 256, 1024], P(('rep', 'node', 'local')), parts along dimension 0
- d_combine: float32 [1024, 8], P(('rep', 'node', 'local')), parts along dimension 0
The draws below stay inside these ranges and needn't reach their ends.
There are 2 independent parts, one for each index of `rep`. The reference program is written for one: setup_inputs(seed, part) draws one part's arguments, and reference() takes and returns one part's arrays. A program takes and returns all parts, laid end to end along the dimension named above; an argument that names none is the same for every part. Nothing has to cross between parts.
Inputs may be any that keep to these rules, and one draw needn't show every extreme that they name: `routes`: each token names 8 different experts lying in exactly 4 node groups (expert e lies in node group e // 4), 2 in each group. The tokens of one device name each node group exactly 32 * 4 // 4 times and each expert exactly 16 times.
All inputs are finite; a program needn't handle non-finite values.
Results may differ from the reference program's by a relative error of at most 0.0055.
Values may be sent and summed in bfloat16 or wider, within the bound.
No kernel may reach another device: no remote copies, remote signals or barrier semaphores. Data moves between devices by JAX's collectives and lax.ppermute only.
A program may use at most 64 MiB of HBM per device.

```python
import math
import jax
import jax.numpy as jnp
from jax import lax

D = 3584
FF = 1024
TOP = 8
TOPNODES = 4
TOK_DEV = 32
EXPERTS = 16
TOKENS = 512
SEND_CAP = 16
SLOTS = 256
N_NODE = 4
N_LOCAL = 4


def draw_routes(key, part):
    key = jax.random.fold_in(key, 11)
    sources = TOKENS // TOK_DEV
    per_node = TOK_DEV * TOPNODES // N_NODE
    per_group = TOP // TOPNODES
    unit_count = per_node * per_group // N_LOCAL
    span_total = TOK_DEV * TOPNODES
    blocks_key = key
    local_iota = jnp.arange(N_LOCAL, dtype=jnp.int32)
    counts = jnp.full((N_LOCAL,), unit_count, jnp.int32)
    bounds = jnp.cumsum(counts).astype(jnp.int32)
    dealt = jnp.arange(per_node * per_group, dtype=jnp.int32)
    rank_of = jnp.sum((dealt[:, None] >= bounds[None, :]).astype(jnp.int32), axis=1)
    node_iota = jnp.arange(N_NODE, dtype=jnp.int32)

    def one_block(block_key):
        keys = jax.random.split(block_key, 4)
        token_order = jax.random.permutation(keys[0], TOK_DEV)
        node_order = jax.random.permutation(keys[1], N_NODE)
        offset = jax.random.randint(keys[2], (), 0, span_total)
        noise = jax.random.randint(keys[3], (N_NODE, N_LOCAL), 0, 100000)
        score = noise * N_LOCAL + local_iota[None, :]
        ranked = jnp.argsort(-score, axis=1)
        local_id = ranked[:, rank_of]
        position = (node_iota[:, None] * per_node - offset + dealt[None, :] % per_node) % span_total
        token_slot = token_order[position % TOK_DEV]
        route_slot = position // TOK_DEV * per_group + dealt[None, :] // per_node
        value = node_order[:, None] * N_LOCAL + local_id
        table = jnp.zeros((TOK_DEV, TOP), jnp.int32)
        return table.at[token_slot.reshape(-1), route_slot.reshape(-1)].set(value.reshape(-1).astype(jnp.int32))
    tables = jax.vmap(one_block)(jax.random.split(blocks_key, sources))
    return tables.reshape(TOKENS, TOP).astype(jnp.int32)


def steps_of(stream_key, dims, cuts, smallest, high):
    def one(axis_at, shards_of):
        heights = jax.random.uniform(jax.random.fold_in(jax.random.fold_in(stream_key, 6), axis_at), (shards_of,), jnp.float32, smallest / len(cuts), high / len(cuts))
        return jnp.repeat(jnp.exp(heights), dims[axis_at] // shards_of).reshape((-1,) + (1,) * (len(dims) - axis_at - 1))

    level = one(*cuts[0])
    for cut in cuts[1:]:
        level = level * one(*cut)
    return level


def bell_draw(stream_key, extent, scale, most, cuts=(), kind=jnp.bfloat16):
    drawn = jax.random.normal(stream_key, extent, jnp.float32) * scale
    if len(cuts) > 0:
        drawn = steps_of(stream_key, extent, cuts, -0.22, 0.18) * drawn
    return jnp.clip(drawn, min=-most, max=most).astype(kind)


def setup_inputs(seed: int = 0, part: int = 0) -> dict:
    arg_keys = jax.random.split(jax.random.key(seed), 6)
    part_splits = jax.random.split(jax.random.fold_in(arg_keys[5], part), 6)
    return {
        "grad_out": bell_draw(part_splits[0], (TOKENS, D), 1.0, 6.0, ((0, 16),)),
        "routes": draw_routes(jax.random.fold_in(jax.random.fold_in(arg_keys[5], part), 71), part),
        "combine": jnp.clip(jnp.exp(math.log(1.0) - 2.9996462 * jax.random.uniform(part_splits[2], (TOKENS, TOP), jnp.float32) ** steps_of(part_splits[2], (TOKENS, TOP), ((0, 16),), -0.2, 0.2)), 0.049804688, 1.0).astype(jnp.bfloat16),
        "hidden_cache": bell_draw(part_splits[3], (EXPERTS, SLOTS, FF), (FF ** -0.5), 0.1875, ((0, 16),)),
        "down_weight": bell_draw(arg_keys[4], (EXPERTS, FF, D), D ** -0.5, 0.09375, ((0, 16),)),
    }


def reference(grad_out, routes, combine, hidden_cache, down_weight):
    tokens_all = grad_out.shape[0]
    slots_total = hidden_cache.shape[1]
    sources = tokens_all // TOK_DEV
    token_ids = jnp.arange(tokens_all, dtype=jnp.int32)
    experts_ids = jnp.arange(hidden_cache.shape[0], dtype=jnp.int32)
    weight_all = combine.astype(jnp.float32)

    def scan_step(totals, inputs):
        expert, cache_rows, weight = inputs
        matches = routes == expert
        hit_count = jnp.sum(matches.astype(jnp.int32), axis=1).astype(jnp.int32)
        weight_tok = jnp.sum(jnp.where(matches, weight_all, jnp.float32(0.0)), axis=1)
        block_hits = hit_count.reshape(sources, TOK_DEV)
        slot_rank = (jnp.cumsum(block_hits, axis=1).astype(jnp.int32) - block_hits).reshape(tokens_all)
        slot_index = ((token_ids // TOK_DEV) * SEND_CAP + slot_rank).astype(jnp.int32)
        slot_index = jnp.where(hit_count > 0, slot_index, slots_total).astype(jnp.int32)
        slot_owner = jnp.zeros((slots_total,), jnp.int32).at[slot_index].set(token_ids, mode="drop")
        slot_scale = jnp.zeros((slots_total,), jnp.float32).at[slot_index].set(weight_tok, mode="drop")
        gathered = grad_out[slot_owner].astype(jnp.float32)
        products = jnp.dot(gathered, weight.astype(jnp.float32).T, precision=lax.Precision.HIGHEST,
                           preferred_element_type=jnp.float32)
        hidden_grad = (slot_scale[:, None] * products).astype(jnp.bfloat16)
        slot_terms = jnp.sum(products * cache_rows.astype(jnp.float32), axis=1)
        safe_index = jnp.minimum(slot_index, slots_total - 1).astype(jnp.int32)
        per_token = jnp.where(hit_count > 0, slot_terms[safe_index], jnp.float32(0.0))
        totals = totals + jnp.where(matches, per_token[:, None], jnp.float32(0.0))
        return totals, hidden_grad

    start = jnp.zeros((tokens_all, routes.shape[1]), jnp.float32)
    d_combine, d_hidden = lax.scan(scan_step, start, (experts_ids, hidden_cache, down_weight))
    return d_hidden, d_combine
```

```python
import functools

import jax
import jax.numpy as jnp
from jax import lax
from jax.experimental import pallas as pl
from jax.experimental.pallas import tpu as pltpu
from jax.sharding import PartitionSpec as P

TOPNODES = 4


def slot_tables(routes, combine, experts_all, capacity):
    onehot = (routes[:, :, None] == lax.iota(jnp.int32, experts_all)[None, None, :]).astype(
        jnp.float32
    )
    hit_mask = jnp.sum(onehot, axis=1)
    weight_te = jnp.einsum("tke,tk->te", onehot, combine.astype(jnp.float32))
    slot_rank = jnp.cumsum(hit_mask, axis=0) - hit_mask
    select = hit_mask[:, :, None] * (
        slot_rank[:, :, None] == lax.iota(jnp.float32, capacity)[None, None, :]
    ).astype(jnp.float32)
    return (onehot, hit_mask, select, select * weight_te[:, :, None])


def routed(grad_out, routes, combine, hidden_cache, down_weight):
    node_count = lax.axis_size("node")
    local_count = lax.axis_size("local")
    experts_all = node_count * local_count
    slots_all = hidden_cache.shape[1]
    capacity = slots_all // experts_all
    tok_rows = grad_out.shape[0]
    width = grad_out.shape[1]
    onehot, hit_mask, select, scaled = slot_tables(routes, combine, experts_all, capacity)
    per_node = tok_rows * TOPNODES // node_count
    node_hit = jnp.max(hit_mask.reshape(tok_rows, node_count, local_count), axis=2)
    node_rank = jnp.cumsum(node_hit, axis=0) - node_hit
    placement = node_hit[:, :, None] * (
        node_rank[:, :, None] == lax.iota(jnp.float32, per_node)[None, None, :]
    ).astype(jnp.float32)
    node_rows = jnp.einsum(
        "tnm,td->nmd", placement.astype(jnp.bfloat16), grad_out, preferred_element_type=jnp.float32
    ).astype(jnp.bfloat16)
    weight_table = jnp.einsum(
        "tnm,tnq->nmq", placement, scaled.reshape(tok_rows, node_count, local_count * capacity)
    ).astype(jnp.bfloat16)
    node_rows, weight_table = (
        lax.all_to_all(node_rows, "node", split_axis=0, concat_axis=0, tiled=True),
        lax.all_to_all(weight_table, "node", split_axis=0, concat_axis=0, tiled=True),
    )
    fan_mask = (weight_table != 0).astype(jnp.bfloat16)
    row_block = jnp.einsum(
        "nmq,nmd->nqd", fan_mask, node_rows, preferred_element_type=jnp.float32
    ).astype(jnp.bfloat16)
    weights = jnp.sum(weight_table.astype(jnp.float32), axis=1).astype(jnp.bfloat16)
    row_block = row_block.reshape(node_count, local_count, capacity, width)
    weights = weights.reshape(node_count, local_count, capacity)
    row_block, weights = (
        lax.all_to_all(row_block, "local", split_axis=1, concat_axis=1, tiled=True),
        lax.all_to_all(weights, "local", split_axis=1, concat_axis=1, tiled=True),
    )
    flat_rows = row_block.reshape(slots_all, width)
    products = lax.dot_general(
        flat_rows, down_weight[0], (((1,), (1,)), ((), ())), preferred_element_type=jnp.float32
    )
    d_hidden = (weights.reshape(slots_all, 1).astype(jnp.float32) * products).astype(jnp.bfloat16)[
        None
    ]
    slot_terms = jnp.sum(products * hidden_cache[0].astype(jnp.float32), axis=1)
    slot_terms = slot_terms.reshape(node_count, local_count, capacity)
    returned = lax.all_to_all(
        lax.all_to_all(slot_terms, "node", split_axis=0, concat_axis=0, tiled=True),
        "local",
        split_axis=1,
        concat_axis=1,
        tiled=True,
    )
    returned = returned.reshape(experts_all, capacity)
    per_expert = jnp.einsum("tec,ec->te", select, returned)
    d_combine = jnp.einsum("tke,te->tk", onehot, per_expert)
    return (d_hidden, d_combine)


LANES = 128
HIGH = 64 * 1024 * 1024


def xor_pairs(nodes, locals_, node_mask, local_mask):
    return [
        (n * locals_ + l, (n ^ node_mask) * locals_ + (l ^ local_mask))
        for n in range(nodes)
        for l in range(locals_)
    ]


def pack_kernel(rows_ref, routes_ref, combine_ref, out_ref):
    width = rows_ref.shape[1]
    top, tokens = routes_ref.shape
    copies = LANES // tokens
    table = jnp.concatenate(
        [routes_ref[...].astype(jnp.float32), combine_ref[...].astype(jnp.float32)], axis=0
    )
    table = jnp.concatenate([table] * copies, axis=1)
    fill = jnp.zeros((rows_ref.shape[0] - 2 * top, LANES), jnp.float32)
    out_ref[:, :width] = rows_ref[...]
    out_ref[:, width:] = jnp.concatenate([table, fill], axis=0).astype(out_ref.dtype)


def expert_kernel(groups, members, place_ref, *refs):
    count = groups * members
    blocks = refs[:count]
    weight_ref, cache_ref, out_ref = refs[count : count + 3]
    term_refs = refs[count + 3 : count + 3 + groups]
    picked, inner, cache_rows = refs[count + 3 + groups :]
    width = weight_ref.shape[1]
    hidden = weight_ref.shape[0]
    tokens = blocks[0].shape[0]
    top = tokens // 4
    capacity = cache_ref.shape[0] // count
    expert = place_ref[0].astype(jnp.float32)
    span = members * tokens
    lane = lax.broadcasted_iota(jnp.int32, (1, span), 1)
    owner = lane // tokens
    earlier = lax.broadcasted_iota(jnp.int32, (span, span), 0)
    later = lax.broadcasted_iota(jnp.int32, (span, span), 1)
    before = ((earlier < later) & (earlier // tokens == later // tokens)).astype(jnp.bfloat16)
    slot_of = lax.broadcasted_iota(jnp.int32, (members * capacity, span), 0).astype(jnp.float32)
    chosen = []
    scales = []
    for j in range(groups):
        mine = blocks[j * members : (j + 1) * members]
        table = jnp.zeros((2 * top, span), jnp.float32)
        for i in range(members):
            part = mine[i][: 2 * top, width:].astype(jnp.float32)
            table = jnp.where(owner == i, part, table)
        match = (table[:top] == expert).astype(jnp.float32)
        hit = jnp.sum(match, axis=0, keepdims=True)
        scale = jnp.sum(match * table[top:], axis=0, keepdims=True)
        rank = jnp.dot(
            jnp.broadcast_to(hit, (top, span)).astype(jnp.bfloat16),
            before,
            preferred_element_type=jnp.float32,
        )[:1]
        target = rank + (owner * capacity).astype(jnp.float32)
        choose = jnp.where((slot_of == target) & (hit > 0), jnp.float32(1), jnp.float32(0))
        chosen.append(choose)
        scales.append(jnp.sum(choose * scale, axis=1, keepdims=True))
        source_rows = jnp.concatenate([mine[i][:, :width] for i in range(members)], axis=0)
        at = j * members * capacity
        picked[at : at + members * capacity, :] = jnp.dot(
            choose.astype(jnp.bfloat16), source_rows, preferred_element_type=jnp.float32
        ).astype(jnp.bfloat16)
        for i in range(members):
            start = pl.multiple_of(place_ref[1 + j * members + i], capacity)
            cache_rows[at + i * capacity : at + (i + 1) * capacity, :] = cache_ref[
                pl.ds(start, capacity), :
            ]
    step = 256
    for f in range(0, hidden, step):
        inner[:, f : f + step] = lax.dot_general(
            picked[...],
            weight_ref[f : f + step, :],
            (((1,), (1,)), ((), ())),
            preferred_element_type=jnp.float32,
        )
    for j in range(groups):
        at = j * members * capacity
        products = inner[at : at + members * capacity, :]
        terms = jnp.sum(
            products * cache_rows[at : at + members * capacity, :].astype(jnp.float32),
            axis=1,
            keepdims=True,
        )
        term_refs[j][...] = jnp.sum(chosen[j] * terms, axis=0, keepdims=True)
        scaled = (scales[j] * products).astype(out_ref.dtype)
        for i in range(members):
            start = pl.multiple_of(place_ref[1 + j * members + i], capacity)
            out_ref[pl.ds(start, capacity), :] = scaled[i * capacity : (i + 1) * capacity]


def finish_kernel(place_ref, routes_ref, *refs):
    out_ref = refs[-1]
    returned = refs[:-1]
    top, tokens = routes_ref.shape
    groups = returned[0].shape[0]
    total = jnp.zeros((top, tokens), jnp.float32)
    routes = routes_ref[...]
    for i in range(len(returned)):
        mine = returned[i][:, i * tokens : (i + 1) * tokens]
        for j in range(groups):
            expert = place_ref[i * groups + j]
            total = total + jnp.where(routes == expert, mine[j : j + 1, :], jnp.float32(0))
    out_ref[...] = total


def exchanged(grad_out, routes, combine, hidden_cache, down_weight):
    nodes = lax.axis_size("node")
    locals_ = lax.axis_size("local")
    sources = nodes * locals_
    tokens, width = grad_out.shape
    hidden = down_weight.shape[1]
    slots = hidden_cache.shape[1]
    capacity = slots // sources
    axes = ("node", "local")
    node = lax.axis_index("node")
    local = lax.axis_index("local")
    vmem = pl.BlockSpec(memory_space=pltpu.VMEM)
    smem = pl.BlockSpec(memory_space=pltpu.SMEM)
    params = pltpu.CompilerParams(vmem_limit_bytes=HIGH * 3 // 4)

    def move(x, node_mask, local_mask):
        return lax.ppermute(x, axes, xor_pairs(nodes, locals_, node_mask, local_mask))

    routes_t = routes.T
    block = pl.pallas_call(
        pack_kernel,
        out_shape=jax.ShapeDtypeStruct((tokens, width + LANES), grad_out.dtype),
        in_specs=[vmem] * 3,
        out_specs=vmem,
    )(grad_out, routes_t, combine.T)

    far = [block] + [move(block, 0, j) for j in range(1, locals_)]
    blocks = []
    for j in range(locals_):
        held = [far[j]]
        bit = nodes // 2
        found = {0: far[j]}
        while bit:
            for at in list(found):
                found[at ^ bit] = move(found[at], bit, 0)
            bit //= 2
        blocks += [found[i] for i in range(nodes)]

    starts = [
        ((node ^ i) * locals_ + (local ^ j)) * capacity for j in range(locals_) for i in range(nodes)
    ]
    place = jnp.stack([node * locals_ + local] + starts).astype(jnp.int32)
    results = pl.pallas_call(
        functools.partial(expert_kernel, locals_, nodes),
        out_shape=[jax.ShapeDtypeStruct((slots, hidden), jnp.bfloat16)]
        + [jax.ShapeDtypeStruct((1, nodes * tokens), jnp.float32)] * locals_,
        in_specs=[smem] + [vmem] * (sources + 2),
        out_specs=[vmem] * (1 + locals_),
        scratch_shapes=[
            pltpu.VMEM((slots, width), jnp.bfloat16),
            pltpu.VMEM((slots, hidden), jnp.float32),
            pltpu.VMEM((slots, hidden), jnp.bfloat16),
        ],
        compiler_params=params,
        cost_estimate=pl.CostEstimate(
            flops=2 * slots * width * hidden * 2, bytes_accessed=2 * hidden * width, transcendentals=0
        ),
    )(place, *blocks, down_weight[0], hidden_cache[0])
    d_hidden, terms = results[0], results[1:]
    back = jnp.concatenate(
        [terms[0]] + [move(terms[j], 0, j) for j in range(1, locals_)], axis=0
    )
    returned = [back] + [move(back, i, 0) for i in range(1, nodes)]
    experts = [
        (node ^ i) * locals_ + (local ^ j) for i in range(nodes) for j in range(locals_)
    ]
    d_combine_t = pl.pallas_call(
        finish_kernel,
        out_shape=jax.ShapeDtypeStruct(routes_t.shape, jnp.float32),
        in_specs=[smem] + [vmem] * (1 + nodes),
        out_specs=vmem,
    )(jnp.stack(experts).astype(jnp.int32), routes_t, *returned)
    return d_hidden[None], d_combine_t.T


def power_of_two(n):
    return n & (n - 1) == 0


def per_device(grad_out, routes, combine, hidden_cache, down_weight):
    nodes = lax.axis_size("node")
    locals_ = lax.axis_size("local")
    tokens, top = routes.shape
    if (
        nodes == TOPNODES
        and power_of_two(nodes)
        and power_of_two(locals_)
        and nodes * tokens == LANES
        and tokens == 4 * top
        and locals_ <= 8
    ):
        return exchanged(grad_out, routes, combine, hidden_cache, down_weight)
    return routed(grad_out, routes, combine, hidden_cache, down_weight)


def solution(mesh):
    placed = (
        P(("rep", "node", "local"), None),
        P(("rep", "node", "local"), None),
        P(("rep", "node", "local"), None),
        P(("rep", "node", "local"), None, None),
        P(("node", "local"), None, None),
    )
    return jax.shard_map(
        per_device,
        mesh=mesh,
        in_specs=placed,
        out_specs=(P(("rep", "node", "local"), None, None), P(("rep", "node", "local"), None)),
        check_vma=False,
    )
```

```python
import functools

import jax
import jax.numpy as jnp
from jax import lax
from jax.experimental import pallas as pl
from jax.experimental.pallas import tpu as pltpu
from jax.sharding import PartitionSpec as P

TOPNODES = 4


def slot_tables(routes, combine, experts_all, capacity):
    onehot = (routes[:, :, None] == lax.iota(jnp.int32, experts_all)[None, None, :]).astype(
        jnp.float32
    )
    hit_mask = jnp.sum(onehot, axis=1)
    weight_te = jnp.einsum("tke,tk->te", onehot, combine.astype(jnp.float32))
    slot_rank = jnp.cumsum(hit_mask, axis=0) - hit_mask
    select = hit_mask[:, :, None] * (
        slot_rank[:, :, None] == lax.iota(jnp.float32, capacity)[None, None, :]
    ).astype(jnp.float32)
    return (onehot, hit_mask, select, select * weight_te[:, :, None])


def routed(grad_out, routes, combine, hidden_cache, down_weight):
    node_count = lax.axis_size("node")
    local_count = lax.axis_size("local")
    experts_all = node_count * local_count
    slots_all = hidden_cache.shape[1]
    capacity = slots_all // experts_all
    tok_rows = grad_out.shape[0]
    width = grad_out.shape[1]
    onehot, hit_mask, select, scaled = slot_tables(routes, combine, experts_all, capacity)
    per_node = tok_rows * TOPNODES // node_count
    node_hit = jnp.max(hit_mask.reshape(tok_rows, node_count, local_count), axis=2)
    node_rank = jnp.cumsum(node_hit, axis=0) - node_hit
    placement = node_hit[:, :, None] * (
        node_rank[:, :, None] == lax.iota(jnp.float32, per_node)[None, None, :]
    ).astype(jnp.float32)
    node_rows = jnp.einsum(
        "tnm,td->nmd", placement.astype(jnp.bfloat16), grad_out, preferred_element_type=jnp.float32
    ).astype(jnp.bfloat16)
    weight_table = jnp.einsum(
        "tnm,tnq->nmq", placement, scaled.reshape(tok_rows, node_count, local_count * capacity)
    ).astype(jnp.bfloat16)
    node_rows, weight_table = (
        lax.all_to_all(node_rows, "node", split_axis=0, concat_axis=0, tiled=True),
        lax.all_to_all(weight_table, "node", split_axis=0, concat_axis=0, tiled=True),
    )
    fan_mask = (weight_table != 0).astype(jnp.bfloat16)
    row_block = jnp.einsum(
        "nmq,nmd->nqd", fan_mask, node_rows, preferred_element_type=jnp.float32
    ).astype(jnp.bfloat16)
    weights = jnp.sum(weight_table.astype(jnp.float32), axis=1).astype(jnp.bfloat16)
    row_block = row_block.reshape(node_count, local_count, capacity, width)
    weights = weights.reshape(node_count, local_count, capacity)
    row_block, weights = (
        lax.all_to_all(row_block, "local", split_axis=1, concat_axis=1, tiled=True),
        lax.all_to_all(weights, "local", split_axis=1, concat_axis=1, tiled=True),
    )
    flat_rows = row_block.reshape(slots_all, width)
    products = lax.dot_general(
        flat_rows, down_weight[0], (((1,), (1,)), ((), ())), preferred_element_type=jnp.float32
    )
    d_hidden = (weights.reshape(slots_all, 1).astype(jnp.float32) * products).astype(jnp.bfloat16)[
        None
    ]
    slot_terms = jnp.sum(products * hidden_cache[0].astype(jnp.float32), axis=1)
    slot_terms = slot_terms.reshape(node_count, local_count, capacity)
    returned = lax.all_to_all(
        lax.all_to_all(slot_terms, "node", split_axis=0, concat_axis=0, tiled=True),
        "local",
        split_axis=1,
        concat_axis=1,
        tiled=True,
    )
    returned = returned.reshape(experts_all, capacity)
    per_expert = jnp.einsum("tec,ec->te", select, returned)
    d_combine = jnp.einsum("tke,te->tk", onehot, per_expert)
    return (d_hidden, d_combine)


LANES = 128
LINE = 4
WORK_BYTES = 16 * 1024 * 1024
CHUNK = 256


def pack_kernel(rows_ref, routes_ref, combine_ref, block_ref, kept_ref):
    top, tokens = routes_ref.shape
    table = jnp.concatenate(
        [routes_ref[...].astype(jnp.float32), combine_ref[...].astype(jnp.float32)], axis=0
    )
    table = jnp.concatenate([table] * (LANES // tokens), axis=1)
    fill = jnp.zeros((rows_ref.shape[0] - 2 * top, LANES), jnp.float32)
    block_ref[:, :LANES] = jnp.concatenate([table, fill], axis=0).astype(rows_ref.dtype)
    block_ref[:, LANES:] = rows_ref[...]
    kept_ref[...] = routes_ref[...]


def pick_rows(blocks, expert, capacity, picked, at):
    tokens = blocks[0].shape[0]
    top = tokens // 4
    span = len(blocks) * tokens
    rows = len(blocks) * capacity
    owner = lax.broadcasted_iota(jnp.int32, (1, span), 1) // tokens
    earlier = lax.broadcasted_iota(jnp.int32, (span, span), 0)
    later = lax.broadcasted_iota(jnp.int32, (span, span), 1)
    before = ((earlier < later) & (earlier // tokens == later // tokens)).astype(jnp.bfloat16)
    table = jnp.zeros((2 * top, span), jnp.float32)
    for i, block in enumerate(blocks):
        table = jnp.where(owner == i, block[: 2 * top, :LANES].astype(jnp.float32), table)
    match = (table[:top] == expert).astype(jnp.float32)
    hit = jnp.sum(match, axis=0, keepdims=True)
    weight = jnp.sum(match * table[top:], axis=0, keepdims=True)
    rank = jnp.dot(
        jnp.broadcast_to(hit, (top, span)).astype(jnp.bfloat16),
        before,
        preferred_element_type=jnp.float32,
    )[:1]
    target = rank + (owner * capacity).astype(jnp.float32)
    slot_of = lax.broadcasted_iota(jnp.int32, (rows, span), 0).astype(jnp.float32)
    choose = jnp.where((slot_of == target) & (hit > 0), jnp.float32(1), jnp.float32(0))
    source_rows = jnp.concatenate([block[:, LANES:] for block in blocks], axis=0)
    picked[at : at + rows, :] = jnp.dot(
        choose.astype(jnp.bfloat16), source_rows, preferred_element_type=jnp.float32
    ).astype(jnp.bfloat16)
    return choose, jnp.sum(choose * weight, axis=1, keepdims=True)


def expert_kernel(masks, members, *refs):
    count = len(masks) * members
    blocks = refs[:count]
    weights, cache, scaled_ref = refs[count : count + 3]
    term_refs = refs[count + 3 : count + 3 + len(masks)]
    picked, chosen, scales = refs[count + 3 + len(masks) :]
    hidden = weights.shape[0]
    node = lax.axis_index("node")
    local = lax.axis_index("local")
    expert = (node * LINE + local).astype(jnp.float32)
    rows = scaled_ref.shape[0] // len(masks)
    capacity = rows // members

    def pick(group, at):
        choose, scale = pick_rows(group, expert, capacity, picked, at)
        chosen[at : at + rows, :] = choose
        scales[at : at + rows, :] = jnp.broadcast_to(scale, (rows, LANES))

    for g in range(len(masks)):
        pick(blocks[g * members : (g + 1) * members], g * rows)

    scale = scales[:, :1]
    terms = jnp.zeros((scaled_ref.shape[0], 1), jnp.float32)
    for c in range(0, hidden, CHUNK):
        part = slice(c, c + CHUNK)
        products = lax.dot_general(
            picked[...], weights[part, :], (((1,), (1,)), ((), ())), preferred_element_type=jnp.float32
        )
        kept = []
        for j in masks:
            for i in range(members):
                source = (node ^ i) * LINE + (local ^ j)
                kept.append(cache[pl.ds(pl.multiple_of(source * capacity, capacity), capacity), part])
        kept = jnp.concatenate(kept, axis=0).astype(jnp.float32)
        terms = terms + jnp.sum(products * kept, axis=1, keepdims=True)
        scaled_ref[:, part] = (scale * products).astype(scaled_ref.dtype)
    spread = chosen[...] * terms
    for g, term_ref in enumerate(term_refs):
        term_ref[...] = jnp.sum(spread[g * rows : (g + 1) * rows], axis=0, keepdims=True)


def place_kernel(masks, members, first_ref, rest_ref, out_ref):
    node = lax.axis_index("node")
    local = lax.axis_index("local")
    capacity = out_ref.shape[0] // (len(masks) * members)
    for g, j in enumerate(masks):
        for i in range(members):
            source = (node ^ i) * LINE + (local ^ j)
            start = pl.multiple_of(source * capacity, capacity)
            at = ((g - 1 if g else 0) * members + i) * capacity
            group_ref = rest_ref if g else first_ref
            out_ref[pl.ds(start, capacity), :] = group_ref[at : at + capacity, :]


def finish_kernel(masks, members, routes_ref, *refs):
    *returned, out_ref = refs
    node = lax.axis_index("node")
    local = lax.axis_index("local")
    routes = routes_ref[...]
    tokens = routes.shape[1]
    total = jnp.zeros(routes.shape, jnp.float32)
    for i in range(members):
        for g, j in enumerate(masks):
            expert = (node ^ i) * LINE + (local ^ j)
            mine = returned[i][g : g + 1, i * tokens : (i + 1) * tokens]
            total = total + jnp.where(routes == expert, mine, jnp.float32(0))
    out_ref[...] = total


def exchanged(grad_out, routes, combine, hidden_cache, down_weight):
    nodes = lax.axis_size("node")
    tokens, width = grad_out.shape
    hidden = down_weight.shape[1]
    slots = hidden_cache.shape[1]
    rows = slots // LINE
    vmem = pl.BlockSpec(memory_space=pltpu.VMEM)

    def move(x, node_mask, local_mask):
        pairs = [
            (n * LINE + l, (n ^ node_mask) * LINE + (l ^ local_mask))
            for n in range(nodes)
            for l in range(LINE)
        ]
        return lax.ppermute(x, ("node", "local"), pairs)

    def after(x, *others):
        return lax.optimization_barrier((x, *others))[0]

    def over_nodes(x, gates=()):
        across = move(x, 2, 0)
        across_beside = move(after(across, *gates), 1, 0)
        return [x, move(x, 1, 0), across, across_beside]

    def multiply(masks, blocks):
        total = rows * len(masks)
        results = pl.pallas_call(
            functools.partial(expert_kernel, masks, nodes),
            out_shape=[jax.ShapeDtypeStruct((total, hidden), jnp.bfloat16)]
            + [jax.ShapeDtypeStruct((1, nodes * tokens), jnp.float32)] * len(masks),
            in_specs=[vmem] * (len(blocks) + 2),
            out_specs=[vmem] * (1 + len(masks)),
            scratch_shapes=[
                pltpu.VMEM((total, width), jnp.bfloat16),
                pltpu.VMEM((total, nodes * tokens), jnp.float32),
                pltpu.VMEM((total, LANES), jnp.float32),
            ],
            compiler_params=pltpu.CompilerParams(vmem_limit_bytes=WORK_BYTES),
            cost_estimate=pl.CostEstimate(flops=1, bytes_accessed=1, transcendentals=0),
        )(*blocks, down_weight[0], hidden_cache[0])
        return results[0], results[1:]

    routes_t = routes.T
    block, kept = pl.pallas_call(
        pack_kernel,
        out_shape=[
            jax.ShapeDtypeStruct((tokens, LANES + width), grad_out.dtype),
            jax.ShapeDtypeStruct(routes_t.shape, routes_t.dtype),
        ],
        in_specs=[vmem] * 3,
        out_specs=[vmem] * 2,
    )(grad_out, routes_t, combine.T)

    masks = (0, 1, 3, 2)
    far = {j: move(block, 0, j) for j in masks[1:]}
    first_rows, first_terms = multiply(masks[:1], over_nodes(block))
    blocks = []
    for j in masks[1:]:
        blocks += over_nodes(far[j], first_terms if j == masks[-1] else ())
    rest_rows, rest_terms = multiply(masks[1:], blocks)

    d_hidden = pl.pallas_call(
        functools.partial(place_kernel, masks, nodes),
        out_shape=jax.ShapeDtypeStruct((slots, hidden), jnp.bfloat16),
        in_specs=[vmem] * 2,
        out_specs=vmem,
    )(first_rows, rest_rows)

    back = list(first_terms) + [move(term, 0, j) for j, term in zip(masks[1:], rest_terms)]
    back = jnp.concatenate(back, axis=0)
    returned = [back] + [move(back, i, 0) for i in range(1, nodes)]
    d_combine_t = pl.pallas_call(
        functools.partial(finish_kernel, masks, nodes),
        out_shape=jax.ShapeDtypeStruct(routes_t.shape, jnp.float32),
        in_specs=[vmem] * (1 + nodes),
        out_specs=vmem,
    )(kept, *returned)
    return d_hidden[None], d_combine_t.T


def per_device(grad_out, routes, combine, hidden_cache, down_weight):
    nodes = lax.axis_size("node")
    locals_ = lax.axis_size("local")
    tokens, top = routes.shape
    if nodes == TOPNODES == 4 and locals_ == LINE and nodes * tokens == LANES and tokens == 4 * top:
        return exchanged(grad_out, routes, combine, hidden_cache, down_weight)
    return routed(grad_out, routes, combine, hidden_cache, down_weight)


def solution(mesh):
    placed = (
        P(("rep", "node", "local"), None),
        P(("rep", "node", "local"), None),
        P(("rep", "node", "local"), None),
        P(("rep", "node", "local"), None, None),
        P(("node", "local"), None, None),
    )
    return jax.shard_map(
        per_device,
        mesh=mesh,
        in_specs=placed,
        out_specs=(P(("rep", "node", "local"), None, None), P(("rep", "node", "local"), None)),
        check_vma=False,
    )
```

```python
import functools

import jax
import jax.numpy as jnp
from jax import lax
from jax.experimental import pallas as pl
from jax.experimental.pallas import tpu as pltpu
from jax.sharding import PartitionSpec as P

TOPNODES = 4


def slot_tables(routes, combine, experts_all, capacity):
    onehot = (routes[:, :, None] == lax.iota(jnp.int32, experts_all)[None, None, :]).astype(
        jnp.float32
    )
    hit_mask = jnp.sum(onehot, axis=1)
    weight_te = jnp.einsum("tke,tk->te", onehot, combine.astype(jnp.float32))
    slot_rank = jnp.cumsum(hit_mask, axis=0) - hit_mask
    select = hit_mask[:, :, None] * (
        slot_rank[:, :, None] == lax.iota(jnp.float32, capacity)[None, None, :]
    ).astype(jnp.float32)
    return (onehot, hit_mask, select, select * weight_te[:, :, None])


def routed(grad_out, routes, combine, hidden_cache, down_weight):
    node_count = lax.axis_size("node")
    local_count = lax.axis_size("local")
    experts_all = node_count * local_count
    slots_all = hidden_cache.shape[1]
    capacity = slots_all // experts_all
    tok_rows = grad_out.shape[0]
    width = grad_out.shape[1]
    onehot, hit_mask, select, scaled = slot_tables(routes, combine, experts_all, capacity)
    per_node = tok_rows * TOPNODES // node_count
    node_hit = jnp.max(hit_mask.reshape(tok_rows, node_count, local_count), axis=2)
    node_rank = jnp.cumsum(node_hit, axis=0) - node_hit
    placement = node_hit[:, :, None] * (
        node_rank[:, :, None] == lax.iota(jnp.float32, per_node)[None, None, :]
    ).astype(jnp.float32)
    node_rows = jnp.einsum(
        "tnm,td->nmd", placement.astype(jnp.bfloat16), grad_out, preferred_element_type=jnp.float32
    ).astype(jnp.bfloat16)
    weight_table = jnp.einsum(
        "tnm,tnq->nmq", placement, scaled.reshape(tok_rows, node_count, local_count * capacity)
    ).astype(jnp.bfloat16)
    node_rows, weight_table = (
        lax.all_to_all(node_rows, "node", split_axis=0, concat_axis=0, tiled=True),
        lax.all_to_all(weight_table, "node", split_axis=0, concat_axis=0, tiled=True),
    )
    fan_mask = (weight_table != 0).astype(jnp.bfloat16)
    row_block = jnp.einsum(
        "nmq,nmd->nqd", fan_mask, node_rows, preferred_element_type=jnp.float32
    ).astype(jnp.bfloat16)
    weights = jnp.sum(weight_table.astype(jnp.float32), axis=1).astype(jnp.bfloat16)
    row_block = row_block.reshape(node_count, local_count, capacity, width)
    weights = weights.reshape(node_count, local_count, capacity)
    row_block, weights = (
        lax.all_to_all(row_block, "local", split_axis=1, concat_axis=1, tiled=True),
        lax.all_to_all(weights, "local", split_axis=1, concat_axis=1, tiled=True),
    )
    flat_rows = row_block.reshape(slots_all, width)
    products = lax.dot_general(
        flat_rows, down_weight[0], (((1,), (1,)), ((), ())), preferred_element_type=jnp.float32
    )
    d_hidden = (weights.reshape(slots_all, 1).astype(jnp.float32) * products).astype(jnp.bfloat16)[
        None
    ]
    slot_terms = jnp.sum(products * hidden_cache[0].astype(jnp.float32), axis=1)
    slot_terms = slot_terms.reshape(node_count, local_count, capacity)
    returned = lax.all_to_all(
        lax.all_to_all(slot_terms, "node", split_axis=0, concat_axis=0, tiled=True),
        "local",
        split_axis=1,
        concat_axis=1,
        tiled=True,
    )
    returned = returned.reshape(experts_all, capacity)
    per_expert = jnp.einsum("tec,ec->te", select, returned)
    d_combine = jnp.einsum("tke,te->tk", onehot, per_expert)
    return (d_hidden, d_combine)


LANES = 128
LINE = 4
WORK_BYTES = 16 * 1024 * 1024
CHUNK = 256


def pack_kernel(rows_hbm, routes_hbm, combine_hbm, block_ref, routes_ref, combine_ref, sems):
    copies = [
        pltpu.make_async_copy(routes_hbm, routes_ref, sems.at[0]),
        pltpu.make_async_copy(combine_hbm, combine_ref, sems.at[1]),
        pltpu.make_async_copy(rows_hbm, block_ref.at[:, LANES:], sems.at[2]),
    ]
    for copy in copies:
        copy.start()
    for copy in copies[:2]:
        copy.wait()
    top, tokens = routes_ref.shape
    table = jnp.concatenate(
        [routes_ref[...].astype(jnp.float32), combine_ref[...].astype(jnp.float32)], axis=0
    )
    table = jnp.concatenate([table] * (LANES // tokens), axis=1)
    fill = jnp.zeros((block_ref.shape[0] - 2 * top, LANES), jnp.float32)
    block_ref[:, :LANES] = jnp.concatenate([table, fill], axis=0).astype(block_ref.dtype)
    copies[2].wait()


def load_kernel(weight_hbm, cache_hbm, weight_ref, cache_ref, sems):
    copies = [
        pltpu.make_async_copy(weight_hbm, weight_ref, sems.at[0]),
        pltpu.make_async_copy(cache_hbm, cache_ref, sems.at[1]),
    ]
    for copy in copies:
        copy.start()
    for copy in copies:
        copy.wait()


def pick_rows(blocks, expert, capacity, picked, at):
    tokens = blocks[0].shape[0]
    top = tokens // 4
    span = len(blocks) * tokens
    rows = len(blocks) * capacity
    owner = lax.broadcasted_iota(jnp.int32, (1, span), 1) // tokens
    earlier = lax.broadcasted_iota(jnp.int32, (span, span), 0)
    later = lax.broadcasted_iota(jnp.int32, (span, span), 1)
    before = ((earlier < later) & (earlier // tokens == later // tokens)).astype(jnp.bfloat16)
    table = jnp.zeros((2 * top, span), jnp.float32)
    for i, block in enumerate(blocks):
        table = jnp.where(owner == i, block[: 2 * top, :LANES].astype(jnp.float32)[:, :span], table)
    match = (table[:top] == expert).astype(jnp.float32)
    hit = jnp.sum(match, axis=0, keepdims=True)
    weight = jnp.sum(match * table[top:], axis=0, keepdims=True)
    rank = jnp.dot(
        jnp.broadcast_to(hit, (top, span)).astype(jnp.bfloat16),
        before,
        preferred_element_type=jnp.float32,
    )[:1]
    target = rank + (owner * capacity).astype(jnp.float32)
    slot_of = lax.broadcasted_iota(jnp.int32, (rows, span), 0).astype(jnp.float32)
    choose = jnp.where((slot_of == target) & (hit > 0), jnp.float32(1), jnp.float32(0))
    source_rows = jnp.concatenate([block[:, LANES:] for block in blocks], axis=0)
    picked[at : at + rows, :] = jnp.dot(
        choose.astype(jnp.bfloat16), source_rows, preferred_element_type=jnp.float32
    ).astype(jnp.bfloat16)
    return choose, jnp.sum(choose * weight, axis=1, keepdims=True)


def source_start(source, capacity):
    i, j = source
    index = (lax.axis_index("node") ^ i) * LINE + (lax.axis_index("local") ^ j)
    return pl.multiple_of(index * capacity, capacity)


def multiply_groups(groups, blocks, weights, cache, picked, rows_ref):
    hidden = weights.shape[0]
    capacity = blocks[0].shape[0] // 2
    expert = (lax.axis_index("node") * LINE + lax.axis_index("local")).astype(jnp.float32)
    chosen, scales, places = [], [], []
    for group in groups:
        at = len(places)
        choose, scale = pick_rows(
            blocks[at : at + len(group)], expert, capacity, picked, at * capacity
        )
        chosen.append(choose)
        scales.append(scale)
        places += [source_start(source, capacity) for source in group]
    scale = jnp.concatenate(scales, axis=0)
    terms = jnp.zeros((len(places) * capacity, 1), jnp.float32)
    for c in range(0, hidden, CHUNK):
        part = slice(c, c + CHUNK)
        products = lax.dot_general(
            picked[...], weights[part, :], (((1,), (1,)), ((), ())), preferred_element_type=jnp.float32
        )
        kept = [cache[pl.ds(place, capacity), part] for place in places]
        kept = jnp.concatenate(kept, axis=0).astype(jnp.float32)
        terms = terms + jnp.sum(products * kept, axis=1, keepdims=True)
        rows_ref[:, part] = (scale * products).astype(rows_ref.dtype)
    results, at = [], 0
    for choose in chosen:
        rows = choose.shape[0]
        results.append(jnp.sum(choose * terms[at : at + rows], axis=0, keepdims=True))
        at += rows
    return results


def expert_kernel(groups, *refs):
    count = sum(len(group) for group in groups)
    blocks = refs[:count]
    weights, cache, rows_ref, *term_refs, picked = refs[count:]
    terms = multiply_groups(groups, blocks, weights, cache, picked, rows_ref)
    for term_ref, term in zip(term_refs, terms):
        term_ref[...] = term


def place_kernel(groups, rows_ref, out_ref):
    sources = [source for group in groups for source in group]
    capacity = out_ref.shape[0] // len(sources)
    for s, source in enumerate(sources):
        out_ref[pl.ds(source_start(source, capacity), capacity), :] = rows_ref[
            s * capacity : (s + 1) * capacity, :
        ]


def exchanged(grad_out, routes, combine, hidden_cache, down_weight):
    nodes = lax.axis_size("node")
    node = lax.axis_index("node")
    local = lax.axis_index("local")
    tokens, width = grad_out.shape
    hidden = down_weight.shape[1]
    slots = hidden_cache.shape[1]
    capacity = slots // (nodes * LINE)
    vmem = pl.BlockSpec(memory_space=pltpu.VMEM)
    hbm = pl.BlockSpec(memory_space=pltpu.HBM)
    params = pltpu.CompilerParams(vmem_limit_bytes=WORK_BYTES)
    free = pl.CostEstimate(flops=1, bytes_accessed=1, transcendentals=0)

    def move(x, node_mask, local_mask):
        pairs = [
            (n * LINE + l, (n ^ node_mask) * LINE + (l ^ local_mask))
            for n in range(nodes)
            for l in range(LINE)
        ]
        return lax.ppermute(x, ("node", "local"), pairs)

    def after(x, *others):
        return lax.optimization_barrier((x, *others))[0]

    def over_nodes(x, *gates):
        across = move(x, 2, 0)
        across_beside = move(after(across, *gates), 1, 0)
        return [x, move(x, 1, 0), across, across_beside]

    def pinned(x, space=pltpu.HBM):
        return pltpu.with_memory_space_constraint(x, space)

    def multiply(groups, blocks):
        rows = len(blocks) * capacity
        return pl.pallas_call(
            functools.partial(expert_kernel, groups),
            out_shape=[jax.ShapeDtypeStruct((rows, hidden), jnp.bfloat16)]
            + [jax.ShapeDtypeStruct((1, len(group) * tokens), jnp.float32) for group in groups],
            in_specs=[vmem] * (len(blocks) + 2),
            out_specs=[vmem] * (1 + len(groups)),
            scratch_shapes=[
                pltpu.VMEM((rows, width), jnp.bfloat16),
            ],
            compiler_params=params,
            cost_estimate=free,
        )(*blocks, pinned(weights, pltpu.VMEM), pinned(cache, pltpu.VMEM))

    routes_t = routes.T
    block = pl.pallas_call(
        pack_kernel,
        out_shape=pltpu.VMEM((tokens, LANES + width), grad_out.dtype),
        in_specs=[hbm] * 3,
        out_specs=vmem,
        scratch_shapes=[
            pltpu.VMEM(routes_t.shape, routes.dtype),
            pltpu.VMEM(routes_t.shape, combine.dtype),
            pltpu.SemaphoreType.DMA((3,)),
        ],
        compiler_params=params,
    )(pinned(grad_out), pinned(routes_t), pinned(combine.T))
    weights, cache = pl.pallas_call(
        load_kernel,
        out_shape=[
            pltpu.VMEM((hidden, width), down_weight.dtype),
            pltpu.VMEM((slots, hidden), hidden_cache.dtype),
        ],
        in_specs=[hbm] * 2,
        out_specs=[vmem] * 2,
        scratch_shapes=[pltpu.SemaphoreType.DMA((2,))],
        compiler_params=params,
        cost_estimate=free,
    )(pinned(down_weight[0]), pinned(hidden_cache[0]))

    order = (1, 3, 2)
    groups = [[(i, j) for i in range(nodes)] for j in (0, *order)]
    far = {j: move(block, 0, j) for j in order}
    blocks = over_nodes(block)
    for j in order:
        blocks += over_nodes(after(far[j], blocks[1]) if j == 1 else far[j], *([cache] if j == 2 else []))
    all_rows, *terms = multiply(groups, blocks)
    d_hidden = pl.pallas_call(
        functools.partial(place_kernel, groups),
        out_shape=jax.ShapeDtypeStruct((slots, hidden), jnp.bfloat16),
        in_specs=[vmem],
        out_specs=vmem,
        compiler_params=params,
        cost_estimate=free,
    )(all_rows)

    back = [terms[0]] + [move(term, 0, j) for j, term in zip(order, terms[1:])]
    back = jnp.concatenate(back, axis=0)
    back, routes_t, node, local = lax.optimization_barrier((back, routes_t, node, local))
    d_combine_t = jnp.zeros(routes_t.shape, jnp.float32)
    for i in range(nodes):
        returned = (move(back, i, 0) if i else back)[:, i * tokens : (i + 1) * tokens]
        for g, j in enumerate((0, *order)):
            expert = (node ^ i) * LINE + (local ^ j)
            d_combine_t += jnp.where(routes_t == expert, returned[g], jnp.float32(0))
    return d_hidden[None], d_combine_t.T


def per_device(grad_out, routes, combine, hidden_cache, down_weight):
    nodes = lax.axis_size("node")
    locals_ = lax.axis_size("local")
    tokens, top = routes.shape
    if nodes == TOPNODES == 4 and locals_ == LINE and nodes * tokens == LANES and tokens == 4 * top:
        return exchanged(grad_out, routes, combine, hidden_cache, down_weight)
    return routed(grad_out, routes, combine, hidden_cache, down_weight)


def solution(mesh):
    placed = (
        P(("rep", "node", "local"), None),
        P(("rep", "node", "local"), None),
        P(("rep", "node", "local"), None),
        P(("rep", "node", "local"), None, None),
        P(("node", "local"), None, None),
    )
    return jax.shard_map(
        per_device,
        mesh=mesh,
        in_specs=placed,
        out_specs=(P(("rep", "node", "local"), None, None), P(("rep", "node", "local"), None)),
        check_vma=False,
    )
```

```python
import functools

import jax
import jax.numpy as jnp
from jax import lax
from jax.experimental import pallas as pl
from jax.experimental.pallas import tpu as pltpu
from jax.sharding import PartitionSpec as P

TOPNODES = 4


def slot_tables(routes, combine, experts_all, capacity):
    onehot = (routes[:, :, None] == lax.iota(jnp.int32, experts_all)[None, None, :]).astype(
        jnp.float32
    )
    hit_mask = jnp.sum(onehot, axis=1)
    weight_te = jnp.einsum("tke,tk->te", onehot, combine.astype(jnp.float32))
    slot_rank = jnp.cumsum(hit_mask, axis=0) - hit_mask
    select = hit_mask[:, :, None] * (
        slot_rank[:, :, None] == lax.iota(jnp.float32, capacity)[None, None, :]
    ).astype(jnp.float32)
    return (onehot, hit_mask, select, select * weight_te[:, :, None])


def routed(grad_out, routes, combine, hidden_cache, down_weight):
    node_count = lax.axis_size("node")
    local_count = lax.axis_size("local")
    experts_all = node_count * local_count
    slots_all = hidden_cache.shape[1]
    capacity = slots_all // experts_all
    tok_rows = grad_out.shape[0]
    width = grad_out.shape[1]
    onehot, hit_mask, select, scaled = slot_tables(routes, combine, experts_all, capacity)
    per_node = tok_rows * TOPNODES // node_count
    node_hit = jnp.max(hit_mask.reshape(tok_rows, node_count, local_count), axis=2)
    node_rank = jnp.cumsum(node_hit, axis=0) - node_hit
    placement = node_hit[:, :, None] * (
        node_rank[:, :, None] == lax.iota(jnp.float32, per_node)[None, None, :]
    ).astype(jnp.float32)
    node_rows = jnp.einsum(
        "tnm,td->nmd", placement.astype(jnp.bfloat16), grad_out, preferred_element_type=jnp.float32
    ).astype(jnp.bfloat16)
    weight_table = jnp.einsum(
        "tnm,tnq->nmq", placement, scaled.reshape(tok_rows, node_count, local_count * capacity)
    ).astype(jnp.bfloat16)
    node_rows, weight_table = (
        lax.all_to_all(node_rows, "node", split_axis=0, concat_axis=0, tiled=True),
        lax.all_to_all(weight_table, "node", split_axis=0, concat_axis=0, tiled=True),
    )
    fan_mask = (weight_table != 0).astype(jnp.bfloat16)
    row_block = jnp.einsum(
        "nmq,nmd->nqd", fan_mask, node_rows, preferred_element_type=jnp.float32
    ).astype(jnp.bfloat16)
    weights = jnp.sum(weight_table.astype(jnp.float32), axis=1).astype(jnp.bfloat16)
    row_block = row_block.reshape(node_count, local_count, capacity, width)
    weights = weights.reshape(node_count, local_count, capacity)
    row_block, weights = (
        lax.all_to_all(row_block, "local", split_axis=1, concat_axis=1, tiled=True),
        lax.all_to_all(weights, "local", split_axis=1, concat_axis=1, tiled=True),
    )
    flat_rows = row_block.reshape(slots_all, width)
    products = lax.dot_general(
        flat_rows, down_weight[0], (((1,), (1,)), ((), ())), preferred_element_type=jnp.float32
    )
    d_hidden = (weights.reshape(slots_all, 1).astype(jnp.float32) * products).astype(jnp.bfloat16)[
        None
    ]
    slot_terms = jnp.sum(products * hidden_cache[0].astype(jnp.float32), axis=1)
    slot_terms = slot_terms.reshape(node_count, local_count, capacity)
    returned = lax.all_to_all(
        lax.all_to_all(slot_terms, "node", split_axis=0, concat_axis=0, tiled=True),
        "local",
        split_axis=1,
        concat_axis=1,
        tiled=True,
    )
    returned = returned.reshape(experts_all, capacity)
    per_expert = jnp.einsum("tec,ec->te", select, returned)
    d_combine = jnp.einsum("tke,te->tk", onehot, per_expert)
    return (d_hidden, d_combine)


LANES = 128
LINE = 4
WORK_BYTES = 16 * 1024 * 1024
CHUNK = 256


def pack_kernel(rows_hbm, routes_hbm, combine_hbm, block_ref, routes_ref, combine_ref, sems):
    copies = [
        pltpu.make_async_copy(routes_hbm, routes_ref, sems.at[0]),
        pltpu.make_async_copy(combine_hbm, combine_ref, sems.at[1]),
        pltpu.make_async_copy(rows_hbm, block_ref.at[:, LANES:], sems.at[2]),
    ]
    for copy in copies:
        copy.start()
    for copy in copies[:2]:
        copy.wait()
    top, tokens = routes_ref.shape
    table = jnp.concatenate(
        [routes_ref[...].astype(jnp.float32), combine_ref[...].astype(jnp.float32)], axis=0
    )
    table = jnp.concatenate([table] * (LANES // tokens), axis=1)
    fill = jnp.zeros((block_ref.shape[0] - 2 * top, LANES), jnp.float32)
    block_ref[:, :LANES] = jnp.concatenate([table, fill], axis=0).astype(block_ref.dtype)
    copies[2].wait()


def load_kernel(weight_hbm, cache_hbm, weight_ref, cache_ref, sems):
    copies = [
        pltpu.make_async_copy(weight_hbm, weight_ref, sems.at[0]),
        pltpu.make_async_copy(cache_hbm, cache_ref, sems.at[1]),
    ]
    for copy in copies:
        copy.start()
    for copy in copies:
        copy.wait()


def pick_rows(blocks, expert, capacity, picked, at):
    tokens = blocks[0].shape[0]
    top = tokens // 4
    span = len(blocks) * tokens
    rows = len(blocks) * capacity
    owner = lax.broadcasted_iota(jnp.int32, (1, span), 1) // tokens
    earlier = lax.broadcasted_iota(jnp.int32, (span, span), 0)
    later = lax.broadcasted_iota(jnp.int32, (span, span), 1)
    before = ((earlier < later) & (earlier // tokens == later // tokens)).astype(jnp.bfloat16)
    table = jnp.zeros((2 * top, span), jnp.float32)
    for i, block in enumerate(blocks):
        table = jnp.where(owner == i, block[: 2 * top, :LANES].astype(jnp.float32)[:, :span], table)
    match = (table[:top] == expert).astype(jnp.float32)
    hit = jnp.sum(match, axis=0, keepdims=True)
    weight = jnp.sum(match * table[top:], axis=0, keepdims=True)
    rank = jnp.dot(
        jnp.broadcast_to(hit, (top, span)).astype(jnp.bfloat16),
        before,
        preferred_element_type=jnp.float32,
    )[:1]
    target = rank + (owner * capacity).astype(jnp.float32)
    slot_of = lax.broadcasted_iota(jnp.int32, (rows, span), 0).astype(jnp.float32)
    choose = jnp.where((slot_of == target) & (hit > 0), jnp.float32(1), jnp.float32(0))
    source_rows = jnp.concatenate([block[:, LANES:] for block in blocks], axis=0)
    picked[at : at + rows, :] = jnp.dot(
        choose.astype(jnp.bfloat16), source_rows, preferred_element_type=jnp.float32
    ).astype(jnp.bfloat16)
    return choose, jnp.sum(choose * weight, axis=1, keepdims=True)


def source_start(source, capacity):
    i, j = source
    index = (lax.axis_index("node") ^ i) * LINE + (lax.axis_index("local") ^ j)
    return pl.multiple_of(index * capacity, capacity)


def multiply_groups(groups, blocks, weights, cache, picked, rows_ref):
    hidden = weights.shape[0]
    capacity = blocks[0].shape[0] // 2
    expert = (lax.axis_index("node") * LINE + lax.axis_index("local")).astype(jnp.float32)
    chosen, scales, places = [], [], []
    for group in groups:
        at = len(places)
        choose, scale = pick_rows(
            blocks[at : at + len(group)], expert, capacity, picked, at * capacity
        )
        chosen.append(choose)
        scales.append(scale)
        places += [source_start(source, capacity) for source in group]
    scale = jnp.concatenate(scales, axis=0)
    terms = jnp.zeros((len(places) * capacity, 1), jnp.float32)
    for c in range(0, hidden, CHUNK):
        part = slice(c, c + CHUNK)
        products = lax.dot_general(
            picked[...], weights[part, :], (((1,), (1,)), ((), ())), preferred_element_type=jnp.float32
        )
        kept = [cache[pl.ds(place, capacity), part] for place in places]
        kept = jnp.concatenate(kept, axis=0).astype(jnp.float32)
        terms = terms + jnp.sum(products * kept, axis=1, keepdims=True)
        rows_ref[:, part] = (scale * products).astype(rows_ref.dtype)
    results, at = [], 0
    for choose in chosen:
        rows = choose.shape[0]
        results.append(jnp.sum(choose * terms[at : at + rows], axis=0, keepdims=True))
        at += rows
    return results


def expert_kernel(groups, *refs):
    count = sum(len(group) for group in groups)
    blocks = refs[:count]
    weights, cache, rows_ref, *term_refs, picked = refs[count:]
    terms = multiply_groups(groups, blocks, weights, cache, picked, rows_ref)
    for term_ref, term in zip(term_refs, terms):
        term_ref[...] = term


def place_kernel(groups, rows_ref, out_ref):
    sources = [source for group in groups for source in group]
    capacity = out_ref.shape[0] // len(sources)
    for s, source in enumerate(sources):
        out_ref[pl.ds(source_start(source, capacity), capacity), :] = rows_ref[
            s * capacity : (s + 1) * capacity, :
        ]


def exchanged(grad_out, routes, combine, hidden_cache, down_weight):
    nodes = lax.axis_size("node")
    node = lax.axis_index("node")
    local = lax.axis_index("local")
    tokens, width = grad_out.shape
    hidden = down_weight.shape[1]
    slots = hidden_cache.shape[1]
    capacity = slots // (nodes * LINE)
    vmem = pl.BlockSpec(memory_space=pltpu.VMEM)
    hbm = pl.BlockSpec(memory_space=pltpu.HBM)
    params = pltpu.CompilerParams(vmem_limit_bytes=WORK_BYTES)
    free = pl.CostEstimate(flops=1, bytes_accessed=1, transcendentals=0)

    def move(x, node_mask, local_mask):
        pairs = [
            (n * LINE + l, (n ^ node_mask) * LINE + (l ^ local_mask))
            for n in range(nodes)
            for l in range(LINE)
        ]
        return lax.ppermute(x, ("node", "local"), pairs)

    def after(x, *others):
        return lax.optimization_barrier((x, *others))[0]

    def over_nodes(x, *gates):
        across = move(x, 2, 0)
        across_beside = move(after(across, *gates), 1, 0)
        return [x, move(x, 1, 0), across, across_beside]

    def pinned(x, space=pltpu.HBM):
        return pltpu.with_memory_space_constraint(x, space)

    def multiply(groups, blocks):
        rows = len(blocks) * capacity
        return pl.pallas_call(
            functools.partial(expert_kernel, groups),
            out_shape=[jax.ShapeDtypeStruct((rows, hidden), jnp.bfloat16)]
            + [jax.ShapeDtypeStruct((1, len(group) * tokens), jnp.float32) for group in groups],
            in_specs=[vmem] * (len(blocks) + 2),
            out_specs=[vmem] * (1 + len(groups)),
            scratch_shapes=[
                pltpu.VMEM((rows, width), jnp.bfloat16),
            ],
            compiler_params=params,
            cost_estimate=free,
        )(*blocks, pinned(weights, pltpu.VMEM), pinned(cache, pltpu.VMEM))

    routes_t = routes.T
    block = pl.pallas_call(
        pack_kernel,
        out_shape=pltpu.VMEM((tokens, LANES + width), grad_out.dtype),
        in_specs=[hbm] * 3,
        out_specs=vmem,
        scratch_shapes=[
            pltpu.VMEM(routes_t.shape, routes.dtype),
            pltpu.VMEM(routes_t.shape, combine.dtype),
            pltpu.SemaphoreType.DMA((3,)),
        ],
        compiler_params=params,
    )(pinned(grad_out), pinned(routes_t), pinned(combine.T))
    weights, cache = pl.pallas_call(
        load_kernel,
        out_shape=[
            pltpu.VMEM((hidden, width), down_weight.dtype),
            pltpu.VMEM((slots, hidden), hidden_cache.dtype),
        ],
        in_specs=[hbm] * 2,
        out_specs=[vmem] * 2,
        scratch_shapes=[pltpu.SemaphoreType.DMA((2,))],
        compiler_params=params,
        cost_estimate=free,
    )(pinned(down_weight[0]), pinned(hidden_cache[0]))

    order = (2, 3, 1)
    groups = [[(i, j) for i in range(nodes)] for j in (0, *order)]
    far = {j: move(block, 0, j) for j in order}
    blocks = over_nodes(block)
    for j in order:
        blocks += over_nodes(after(far[j], blocks[1]) if j == 1 else far[j], *([cache] if j == 3 else []))
    all_rows, *terms = multiply(groups, blocks)
    d_hidden = pl.pallas_call(
        functools.partial(place_kernel, groups),
        out_shape=jax.ShapeDtypeStruct((slots, hidden), jnp.bfloat16),
        in_specs=[vmem],
        out_specs=vmem,
        compiler_params=params,
        cost_estimate=free,
    )(all_rows)

    back = [terms[0]] + [move(term, 0, j) for j, term in zip(order, terms[1:])]
    back = jnp.concatenate(back, axis=0)
    back, routes_t, node, local = lax.optimization_barrier((back, routes_t, node, local))
    d_combine_t = jnp.zeros(routes_t.shape, jnp.float32)
    for i in range(nodes):
        returned = (move(back, i, 0) if i else back)[:, i * tokens : (i + 1) * tokens]
        for g, j in enumerate((0, *order)):
            expert = (node ^ i) * LINE + (local ^ j)
            d_combine_t += jnp.where(routes_t == expert, returned[g], jnp.float32(0))
    return d_hidden[None], d_combine_t.T


def per_device(grad_out, routes, combine, hidden_cache, down_weight):
    nodes = lax.axis_size("node")
    locals_ = lax.axis_size("local")
    tokens, top = routes.shape
    if nodes == TOPNODES == 4 and locals_ == LINE and nodes * tokens == LANES and tokens == 4 * top:
        return exchanged(grad_out, routes, combine, hidden_cache, down_weight)
    return routed(grad_out, routes, combine, hidden_cache, down_weight)


def solution(mesh):
    placed = (
        P(("rep", "node", "local"), None),
        P(("rep", "node", "local"), None),
        P(("rep", "node", "local"), None),
        P(("rep", "node", "local"), None, None),
        P(("node", "local"), None, None),
    )
    return jax.shard_map(
        per_device,
        mesh=mesh,
        in_specs=placed,
        out_specs=(P(("rep", "node", "local"), None, None), P(("rep", "node", "local"), None)),
        check_vma=False,
    )
```

```python
import functools

import jax
import jax.numpy as jnp
from jax import lax
from jax.experimental import pallas as pl
from jax.experimental.pallas import tpu as pltpu
from jax.sharding import PartitionSpec as P

TOPNODES = 4


def slot_tables(routes, combine, experts_all, capacity):
    onehot = (routes[:, :, None] == lax.iota(jnp.int32, experts_all)[None, None, :]).astype(
        jnp.float32
    )
    hit_mask = jnp.sum(onehot, axis=1)
    weight_te = jnp.einsum("tke,tk->te", onehot, combine.astype(jnp.float32))
    slot_rank = jnp.cumsum(hit_mask, axis=0) - hit_mask
    select = hit_mask[:, :, None] * (
        slot_rank[:, :, None] == lax.iota(jnp.float32, capacity)[None, None, :]
    ).astype(jnp.float32)
    return (onehot, hit_mask, select, select * weight_te[:, :, None])


def routed(grad_out, routes, combine, hidden_cache, down_weight):
    node_count = lax.axis_size("node")
    local_count = lax.axis_size("local")
    experts_all = node_count * local_count
    slots_all = hidden_cache.shape[1]
    capacity = slots_all // experts_all
    tok_rows = grad_out.shape[0]
    width = grad_out.shape[1]
    onehot, hit_mask, select, scaled = slot_tables(routes, combine, experts_all, capacity)
    per_node = tok_rows * TOPNODES // node_count
    node_hit = jnp.max(hit_mask.reshape(tok_rows, node_count, local_count), axis=2)
    node_rank = jnp.cumsum(node_hit, axis=0) - node_hit
    placement = node_hit[:, :, None] * (
        node_rank[:, :, None] == lax.iota(jnp.float32, per_node)[None, None, :]
    ).astype(jnp.float32)
    node_rows = jnp.einsum(
        "tnm,td->nmd", placement.astype(jnp.bfloat16), grad_out, preferred_element_type=jnp.float32
    ).astype(jnp.bfloat16)
    weight_table = jnp.einsum(
        "tnm,tnq->nmq", placement, scaled.reshape(tok_rows, node_count, local_count * capacity)
    ).astype(jnp.bfloat16)
    node_rows, weight_table = (
        lax.all_to_all(node_rows, "node", split_axis=0, concat_axis=0, tiled=True),
        lax.all_to_all(weight_table, "node", split_axis=0, concat_axis=0, tiled=True),
    )
    fan_mask = (weight_table != 0).astype(jnp.bfloat16)
    row_block = jnp.einsum(
        "nmq,nmd->nqd", fan_mask, node_rows, preferred_element_type=jnp.float32
    ).astype(jnp.bfloat16)
    weights = jnp.sum(weight_table.astype(jnp.float32), axis=1).astype(jnp.bfloat16)
    row_block = row_block.reshape(node_count, local_count, capacity, width)
    weights = weights.reshape(node_count, local_count, capacity)
    row_block, weights = (
        lax.all_to_all(row_block, "local", split_axis=1, concat_axis=1, tiled=True),
        lax.all_to_all(weights, "local", split_axis=1, concat_axis=1, tiled=True),
    )
    flat_rows = row_block.reshape(slots_all, width)
    products = lax.dot_general(
        flat_rows, down_weight[0], (((1,), (1,)), ((), ())), preferred_element_type=jnp.float32
    )
    d_hidden = (weights.reshape(slots_all, 1).astype(jnp.float32) * products).astype(jnp.bfloat16)[
        None
    ]
    slot_terms = jnp.sum(products * hidden_cache[0].astype(jnp.float32), axis=1)
    slot_terms = slot_terms.reshape(node_count, local_count, capacity)
    returned = lax.all_to_all(
        lax.all_to_all(slot_terms, "node", split_axis=0, concat_axis=0, tiled=True),
        "local",
        split_axis=1,
        concat_axis=1,
        tiled=True,
    )
    returned = returned.reshape(experts_all, capacity)
    per_expert = jnp.einsum("tec,ec->te", select, returned)
    d_combine = jnp.einsum("tke,te->tk", onehot, per_expert)
    return (d_hidden, d_combine)


LANES = 128
LINE = 4
WORK_BYTES = 16 * 1024 * 1024
CHUNK = 256


def pack_kernel(rows_hbm, routes_hbm, combine_hbm, block_ref, routes_ref, combine_ref, sems):
    copies = [
        pltpu.make_async_copy(routes_hbm, routes_ref, sems.at[0]),
        pltpu.make_async_copy(combine_hbm, combine_ref, sems.at[1]),
        pltpu.make_async_copy(rows_hbm, block_ref.at[:, LANES:], sems.at[2]),
    ]
    for copy in copies:
        copy.start()
    for copy in copies[:2]:
        copy.wait()
    top, tokens = routes_ref.shape
    table = jnp.concatenate(
        [routes_ref[...].astype(jnp.float32), combine_ref[...].astype(jnp.float32)], axis=0
    )
    table = jnp.concatenate([table] * (LANES // tokens), axis=1)
    fill = jnp.zeros((block_ref.shape[0] - 2 * top, LANES), jnp.float32)
    block_ref[:, :LANES] = jnp.concatenate([table, fill], axis=0).astype(block_ref.dtype)
    copies[2].wait()


def load_kernel(weight_hbm, cache_hbm, weight_ref, cache_ref, sems):
    copies = [
        pltpu.make_async_copy(weight_hbm, weight_ref, sems.at[0]),
        pltpu.make_async_copy(cache_hbm, cache_ref, sems.at[1]),
    ]
    for copy in copies:
        copy.start()
    for copy in copies:
        copy.wait()


def pick_rows(blocks, expert, capacity, picked, at):
    tokens = blocks[0].shape[0]
    top = tokens // 4
    span = len(blocks) * tokens
    rows = len(blocks) * capacity
    owner = lax.broadcasted_iota(jnp.int32, (1, span), 1) // tokens
    earlier = lax.broadcasted_iota(jnp.int32, (span, span), 0)
    later = lax.broadcasted_iota(jnp.int32, (span, span), 1)
    before = ((earlier < later) & (earlier // tokens == later // tokens)).astype(jnp.bfloat16)
    table = jnp.zeros((2 * top, span), jnp.float32)
    for i, block in enumerate(blocks):
        table = jnp.where(owner == i, block[: 2 * top, :LANES].astype(jnp.float32)[:, :span], table)
    match = (table[:top] == expert).astype(jnp.float32)
    hit = jnp.sum(match, axis=0, keepdims=True)
    weight = jnp.sum(match * table[top:], axis=0, keepdims=True)
    rank = jnp.dot(
        jnp.broadcast_to(hit, (top, span)).astype(jnp.bfloat16),
        before,
        preferred_element_type=jnp.float32,
    )[:1]
    target = rank + (owner * capacity).astype(jnp.float32)
    slot_of = lax.broadcasted_iota(jnp.int32, (rows, span), 0).astype(jnp.float32)
    choose = jnp.where((slot_of == target) & (hit > 0), jnp.float32(1), jnp.float32(0))
    source_rows = jnp.concatenate([block[:, LANES:] for block in blocks], axis=0)
    picked[at : at + rows, :] = jnp.dot(
        choose.astype(jnp.bfloat16), source_rows, preferred_element_type=jnp.float32
    ).astype(jnp.bfloat16)
    return choose, jnp.sum(choose * weight, axis=1, keepdims=True)


def source_start(source, capacity):
    i, j = source
    index = (lax.axis_index("node") ^ i) * LINE + (lax.axis_index("local") ^ j)
    return pl.multiple_of(index * capacity, capacity)


def pick_kernel(groups, *refs):
    *blocks, picked, chosen_ref, scale_ref = refs
    expert = (lax.axis_index("node") * LINE + lax.axis_index("local")).astype(jnp.float32)
    capacity = blocks[0].shape[0] // 2
    at = 0
    for g, group in enumerate(groups):
        mine = blocks[g * len(group) : (g + 1) * len(group)]
        choose, scale = pick_rows(mine, expert, capacity, picked, at)
        rows = choose.shape[0]
        chosen_ref[at : at + rows, :] = choose
        scale_ref[at : at + rows, :] = jnp.broadcast_to(scale, (rows, LANES))
        at += rows


def expert_kernel(groups, *refs):
    members = len(groups[-1])
    chosen_ref, scale_ref, weights, cache, _ = refs[:5]
    blocks, rows_ref = refs[5 : 5 + members], refs[5 + members]
    term_refs, picked = refs[6 + members : -1], refs[-1]
    hidden = weights.shape[0]
    capacity = blocks[0].shape[0] // 2
    expert = (lax.axis_index("node") * LINE + lax.axis_index("local")).astype(jnp.float32)
    early = chosen_ref.shape[0]
    choose, scale = pick_rows(blocks, expert, capacity, picked, early)
    scale = jnp.concatenate([scale_ref[:, :1], scale], axis=0)
    choose = jnp.concatenate([chosen_ref[...], choose], axis=0)
    places = [source_start(source, capacity) for group in groups for source in group]
    terms = jnp.zeros((len(places) * capacity, 1), jnp.float32)
    for c in range(0, hidden, CHUNK):
        part = slice(c, c + CHUNK)
        products = lax.dot_general(
            picked[...], weights[part, :], (((1,), (1,)), ((), ())), preferred_element_type=jnp.float32
        )
        kept = [cache[pl.ds(place, capacity), part] for place in places]
        kept = jnp.concatenate(kept, axis=0).astype(jnp.float32)
        terms = terms + jnp.sum(products * kept, axis=1, keepdims=True)
        rows_ref[:, part] = (scale * products).astype(rows_ref.dtype)
    spread = choose * terms
    rows = members * capacity
    for g, term_ref in enumerate(term_refs):
        term_ref[...] = jnp.sum(spread[g * rows : (g + 1) * rows], axis=0, keepdims=True)


def place_kernel(groups, rows_ref, out_ref):
    sources = [source for group in groups for source in group]
    capacity = out_ref.shape[0] // len(sources)
    for s, source in enumerate(sources):
        out_ref[pl.ds(source_start(source, capacity), capacity), :] = rows_ref[
            s * capacity : (s + 1) * capacity, :
        ]


def exchanged(grad_out, routes, combine, hidden_cache, down_weight):
    nodes = lax.axis_size("node")
    node = lax.axis_index("node")
    local = lax.axis_index("local")
    tokens, width = grad_out.shape
    hidden = down_weight.shape[1]
    slots = hidden_cache.shape[1]
    capacity = slots // (nodes * LINE)
    vmem = pl.BlockSpec(memory_space=pltpu.VMEM)
    hbm = pl.BlockSpec(memory_space=pltpu.HBM)
    params = pltpu.CompilerParams(vmem_limit_bytes=WORK_BYTES)
    free = pl.CostEstimate(flops=1, bytes_accessed=1, transcendentals=0)

    def move(x, node_mask, local_mask):
        pairs = [
            (n * LINE + l, (n ^ node_mask) * LINE + (l ^ local_mask))
            for n in range(nodes)
            for l in range(LINE)
        ]
        return lax.ppermute(x, ("node", "local"), pairs)

    def after(x, *others):
        return lax.optimization_barrier((x, *others))[0]

    def over_nodes(x, *gates):
        across = move(x, 2, 0)
        across_beside = move(after(across, *gates), 1, 0)
        return [x, move(x, 1, 0), across, across_beside]

    def pinned(x, space=pltpu.HBM):
        return pltpu.with_memory_space_constraint(x, space)

    routes_t = routes.T
    block = pl.pallas_call(
        pack_kernel,
        out_shape=pltpu.VMEM((tokens, LANES + width), grad_out.dtype),
        in_specs=[hbm] * 3,
        out_specs=vmem,
        scratch_shapes=[
            pltpu.VMEM(routes_t.shape, routes.dtype),
            pltpu.VMEM(routes_t.shape, combine.dtype),
            pltpu.SemaphoreType.DMA((3,)),
        ],
        compiler_params=params,
    )(pinned(grad_out), pinned(routes_t), pinned(combine.T))
    weights, cache = pl.pallas_call(
        load_kernel,
        out_shape=[
            pltpu.VMEM((hidden, width), down_weight.dtype),
            pltpu.VMEM((slots, hidden), hidden_cache.dtype),
        ],
        in_specs=[hbm] * 2,
        out_specs=[vmem] * 2,
        scratch_shapes=[pltpu.SemaphoreType.DMA((2,))],
        compiler_params=params,
        cost_estimate=free,
    )(pinned(down_weight[0]), pinned(hidden_cache[0]))

    early, late = (3, 1, 0), 2
    order = (*[j for j in early if j], late)
    groups = [[(i, j) for i in range(nodes)] for j in (*early, late)]
    far = {j: move(block, 0, j) for j in (2, 3, 1)}
    blocks = []
    for j in early:
        blocks += over_nodes(far[j] if j else block, *([cache] if j == early[0] else []))
    rows = len(blocks) * capacity
    picked, chosen, scales = pl.pallas_call(
        functools.partial(pick_kernel, groups[:-1]),
        out_shape=[
            pltpu.VMEM((slots, width), jnp.bfloat16),
            pltpu.VMEM((rows, LANES), jnp.float32),
            pltpu.VMEM((rows, LANES), jnp.float32),
        ],
        in_specs=[vmem] * len(blocks),
        out_specs=[vmem] * 3,
        compiler_params=params,
        cost_estimate=pl.CostEstimate(
            flops=2 * rows * nodes * tokens * width, bytes_accessed=1 << 22, transcendentals=0
        ),
    )(*blocks)
    blocks = over_nodes(far[late])
    held = [chosen, scales, weights, cache, picked]
    all_rows, *terms = pl.pallas_call(
        functools.partial(expert_kernel, groups),
        out_shape=[jax.ShapeDtypeStruct((slots, hidden), jnp.bfloat16)]
        + [jax.ShapeDtypeStruct((1, nodes * tokens), jnp.float32)] * LINE
        + [pltpu.VMEM(picked.shape, picked.dtype)],
        in_specs=[vmem] * (nodes + len(held)),
        out_specs=[vmem] * (2 + LINE),
        input_output_aliases={len(held) - 1: 1 + LINE},
        compiler_params=params,
        cost_estimate=free,
    )(*[pinned(x, pltpu.VMEM) for x in held], *blocks)
    terms = dict(zip((*early, late), terms))
    d_hidden = pl.pallas_call(
        functools.partial(place_kernel, groups),
        out_shape=jax.ShapeDtypeStruct((slots, hidden), jnp.bfloat16),
        in_specs=[vmem],
        out_specs=vmem,
        compiler_params=params,
        cost_estimate=free,
    )(all_rows)

    back = [move(terms[j], 0, j) if j else terms[j] for j in (0, *order)]
    back = jnp.concatenate(back, axis=0)
    back, routes_t, node, local = lax.optimization_barrier((back, routes_t, node, local))
    d_combine_t = jnp.zeros(routes_t.shape, jnp.float32)
    for i in range(nodes):
        returned = (move(back, i, 0) if i else back)[:, i * tokens : (i + 1) * tokens]
        for g, j in enumerate((0, *order)):
            expert = (node ^ i) * LINE + (local ^ j)
            d_combine_t += jnp.where(routes_t == expert, returned[g], jnp.float32(0))
    return d_hidden[None], d_combine_t.T


def per_device(grad_out, routes, combine, hidden_cache, down_weight):
    nodes = lax.axis_size("node")
    locals_ = lax.axis_size("local")
    tokens, top = routes.shape
    fits = nodes * tokens == LANES and tokens == 4 * top and hidden_cache.shape[1] == 8 * tokens
    if nodes == TOPNODES == 4 and locals_ == LINE and fits:
        return exchanged(grad_out, routes, combine, hidden_cache, down_weight)
    return routed(grad_out, routes, combine, hidden_cache, down_weight)


def solution(mesh):
    placed = (
        P(("rep", "node", "local"), None),
        P(("rep", "node", "local"), None),
        P(("rep", "node", "local"), None),
        P(("rep", "node", "local"), None, None),
        P(("node", "local"), None, None),
    )
    return jax.shard_map(
        per_device,
        mesh=mesh,
        in_specs=placed,
        out_specs=(P(("rep", "node", "local"), None, None), P(("rep", "node", "local"), None)),
        check_vma=False,
    )
```

```python
import functools

import jax
import jax.numpy as jnp
from jax import lax
from jax.experimental import pallas as pl
from jax.experimental.pallas import tpu as pltpu
from jax.sharding import PartitionSpec as P

TOPNODES = 4


def slot_tables(routes, combine, experts_all, capacity):
    onehot = (routes[:, :, None] == lax.iota(jnp.int32, experts_all)[None, None, :]).astype(
        jnp.float32
    )
    hit_mask = jnp.sum(onehot, axis=1)
    weight_te = jnp.einsum("tke,tk->te", onehot, combine.astype(jnp.float32))
    slot_rank = jnp.cumsum(hit_mask, axis=0) - hit_mask
    select = hit_mask[:, :, None] * (
        slot_rank[:, :, None] == lax.iota(jnp.float32, capacity)[None, None, :]
    ).astype(jnp.float32)
    return (onehot, hit_mask, select, select * weight_te[:, :, None])


def routed(grad_out, routes, combine, hidden_cache, down_weight):
    node_count = lax.axis_size("node")
    local_count = lax.axis_size("local")
    experts_all = node_count * local_count
    slots_all = hidden_cache.shape[1]
    capacity = slots_all // experts_all
    tok_rows = grad_out.shape[0]
    width = grad_out.shape[1]
    onehot, hit_mask, select, scaled = slot_tables(routes, combine, experts_all, capacity)
    per_node = tok_rows * TOPNODES // node_count
    node_hit = jnp.max(hit_mask.reshape(tok_rows, node_count, local_count), axis=2)
    node_rank = jnp.cumsum(node_hit, axis=0) - node_hit
    placement = node_hit[:, :, None] * (
        node_rank[:, :, None] == lax.iota(jnp.float32, per_node)[None, None, :]
    ).astype(jnp.float32)
    node_rows = jnp.einsum(
        "tnm,td->nmd", placement.astype(jnp.bfloat16), grad_out, preferred_element_type=jnp.float32
    ).astype(jnp.bfloat16)
    weight_table = jnp.einsum(
        "tnm,tnq->nmq", placement, scaled.reshape(tok_rows, node_count, local_count * capacity)
    ).astype(jnp.bfloat16)
    node_rows, weight_table = (
        lax.all_to_all(node_rows, "node", split_axis=0, concat_axis=0, tiled=True),
        lax.all_to_all(weight_table, "node", split_axis=0, concat_axis=0, tiled=True),
    )
    fan_mask = (weight_table != 0).astype(jnp.bfloat16)
    row_block = jnp.einsum(
        "nmq,nmd->nqd", fan_mask, node_rows, preferred_element_type=jnp.float32
    ).astype(jnp.bfloat16)
    weights = jnp.sum(weight_table.astype(jnp.float32), axis=1).astype(jnp.bfloat16)
    row_block = row_block.reshape(node_count, local_count, capacity, width)
    weights = weights.reshape(node_count, local_count, capacity)
    row_block, weights = (
        lax.all_to_all(row_block, "local", split_axis=1, concat_axis=1, tiled=True),
        lax.all_to_all(weights, "local", split_axis=1, concat_axis=1, tiled=True),
    )
    flat_rows = row_block.reshape(slots_all, width)
    products = lax.dot_general(
        flat_rows, down_weight[0], (((1,), (1,)), ((), ())), preferred_element_type=jnp.float32
    )
    d_hidden = (weights.reshape(slots_all, 1).astype(jnp.float32) * products).astype(jnp.bfloat16)[
        None
    ]
    slot_terms = jnp.sum(products * hidden_cache[0].astype(jnp.float32), axis=1)
    slot_terms = slot_terms.reshape(node_count, local_count, capacity)
    returned = lax.all_to_all(
        lax.all_to_all(slot_terms, "node", split_axis=0, concat_axis=0, tiled=True),
        "local",
        split_axis=1,
        concat_axis=1,
        tiled=True,
    )
    returned = returned.reshape(experts_all, capacity)
    per_expert = jnp.einsum("tec,ec->te", select, returned)
    d_combine = jnp.einsum("tke,te->tk", onehot, per_expert)
    return (d_hidden, d_combine)


LANES = 128
LINE = 4
WORK_BYTES = 16 * 1024 * 1024
CHUNK = 512


def pack_kernel(rows_hbm, routes_hbm, combine_hbm, block_ref, routes_ref, combine_ref, sems):
    copies = [
        pltpu.make_async_copy(routes_hbm, routes_ref, sems.at[0]),
        pltpu.make_async_copy(combine_hbm, combine_ref, sems.at[1]),
        pltpu.make_async_copy(rows_hbm, block_ref.at[:, LANES:], sems.at[2]),
    ]
    for copy in copies:
        copy.start()
    for copy in copies[:2]:
        copy.wait()
    top, tokens = routes_ref.shape
    table = jnp.concatenate(
        [routes_ref[...].astype(jnp.float32), combine_ref[...].astype(jnp.float32)], axis=0
    )
    table = jnp.concatenate([table] * (LANES // tokens), axis=1)
    fill = jnp.zeros((block_ref.shape[0] - 2 * top, LANES), jnp.float32)
    block_ref[:, :LANES] = jnp.concatenate([table, fill], axis=0).astype(block_ref.dtype)
    copies[2].wait()


def load_kernel(weight_hbm, cache_hbm, weight_ref, cache_ref, sems):
    copies = [
        pltpu.make_async_copy(weight_hbm, weight_ref, sems.at[0]),
        pltpu.make_async_copy(cache_hbm, cache_ref, sems.at[1]),
    ]
    for copy in copies:
        copy.start()
    for copy in copies:
        copy.wait()


def pick_rows(blocks, expert, capacity, picked, at):
    tokens = blocks[0].shape[0]
    top = tokens // 4
    span = len(blocks) * tokens
    rows = len(blocks) * capacity
    owner = lax.broadcasted_iota(jnp.int32, (1, span), 1) // tokens
    earlier = lax.broadcasted_iota(jnp.int32, (span, span), 0)
    later = lax.broadcasted_iota(jnp.int32, (span, span), 1)
    before = ((earlier < later) & (earlier // tokens == later // tokens)).astype(jnp.bfloat16)
    table = jnp.zeros((2 * top, span), jnp.float32)
    for i, block in enumerate(blocks):
        table = jnp.where(owner == i, block[: 2 * top, :LANES].astype(jnp.float32)[:, :span], table)
    match = (table[:top] == expert).astype(jnp.float32)
    hit = jnp.sum(match, axis=0, keepdims=True)
    weight = jnp.sum(match * table[top:], axis=0, keepdims=True)
    rank = jnp.dot(
        jnp.broadcast_to(hit, (top, span)).astype(jnp.bfloat16),
        before,
        preferred_element_type=jnp.float32,
    )[:1]
    target = rank + (owner * capacity).astype(jnp.float32)
    slot_of = lax.broadcasted_iota(jnp.int32, (rows, span), 0).astype(jnp.float32)
    choose = jnp.where((slot_of == target) & (hit > 0), jnp.float32(1), jnp.float32(0))
    source_rows = jnp.concatenate([block[:, LANES:] for block in blocks], axis=0)
    picked[at : at + rows, :] = jnp.dot(
        choose.astype(jnp.bfloat16), source_rows, preferred_element_type=jnp.float32
    ).astype(jnp.bfloat16)
    return choose, jnp.sum(choose * weight, axis=1, keepdims=True)


def source_start(source, capacity):
    i, j = source
    index = (lax.axis_index("node") ^ i) * LINE + (lax.axis_index("local") ^ j)
    return pl.multiple_of(index * capacity, capacity)


def pick_kernel(groups, *refs):
    *blocks, picked, chosen_ref, scale_ref = refs
    expert = (lax.axis_index("node") * LINE + lax.axis_index("local")).astype(jnp.float32)
    capacity = blocks[0].shape[0] // 2
    at = 0
    for g, group in enumerate(groups):
        mine = blocks[g * len(group) : (g + 1) * len(group)]
        choose, scale = pick_rows(mine, expert, capacity, picked, at)
        rows = choose.shape[0]
        chosen_ref[at : at + rows, :] = choose
        scale_ref[at : at + rows, :] = jnp.broadcast_to(scale, (rows, LANES))
        at += rows


def expert_kernel(groups, *refs):
    members = len(groups[-1])
    chosen_ref, scale_ref, weights, cache, _ = refs[:5]
    blocks, rows_ref = refs[5 : 5 + members], refs[5 + members]
    term_refs, picked = refs[6 + members : -1], refs[-1]
    hidden = weights.shape[0]
    capacity = blocks[0].shape[0] // 2
    expert = (lax.axis_index("node") * LINE + lax.axis_index("local")).astype(jnp.float32)
    early = chosen_ref.shape[0]
    choose, scale = pick_rows(blocks, expert, capacity, picked, early)
    scale = jnp.concatenate([scale_ref[:, :1], scale], axis=0)
    choose = jnp.concatenate([chosen_ref[...], choose], axis=0)
    places = [source_start(source, capacity) for group in groups for source in group]
    terms = jnp.zeros((len(places) * capacity, 1), jnp.float32)
    for c in range(0, hidden, CHUNK):
        part = slice(c, c + CHUNK)
        products = lax.dot_general(
            picked[...], weights[part, :], (((1,), (1,)), ((), ())), preferred_element_type=jnp.float32
        )
        kept = [cache[pl.ds(place, capacity), part] for place in places]
        kept = jnp.concatenate(kept, axis=0).astype(jnp.float32)
        terms = terms + jnp.sum(products * kept, axis=1, keepdims=True)
        rows_ref[:, part] = (scale * products).astype(rows_ref.dtype)
    spread = choose * terms
    rows = members * capacity
    for g, term_ref in enumerate(term_refs):
        term_ref[...] = jnp.sum(spread[g * rows : (g + 1) * rows], axis=0, keepdims=True)


def place_kernel(groups, rows_ref, out_ref):
    sources = [source for group in groups for source in group]
    capacity = out_ref.shape[0] // len(sources)
    for s, source in enumerate(sources):
        out_ref[pl.ds(source_start(source, capacity), capacity), :] = rows_ref[
            s * capacity : (s + 1) * capacity, :
        ]


def exchanged(grad_out, routes, combine, hidden_cache, down_weight):
    nodes = lax.axis_size("node")
    node = lax.axis_index("node")
    local = lax.axis_index("local")
    tokens, width = grad_out.shape
    hidden = down_weight.shape[1]
    slots = hidden_cache.shape[1]
    capacity = slots // (nodes * LINE)
    vmem = pl.BlockSpec(memory_space=pltpu.VMEM)
    hbm = pl.BlockSpec(memory_space=pltpu.HBM)
    params = pltpu.CompilerParams(vmem_limit_bytes=WORK_BYTES)
    free = pl.CostEstimate(flops=1, bytes_accessed=1, transcendentals=0)

    def move(x, node_mask, local_mask):
        pairs = [
            (n * LINE + l, (n ^ node_mask) * LINE + (l ^ local_mask))
            for n in range(nodes)
            for l in range(LINE)
        ]
        return lax.ppermute(x, ("node", "local"), pairs)

    def after(x, *others):
        return lax.optimization_barrier((x, *others))[0]

    def over_nodes(x, *gates):
        across = move(x, 2, 0)
        across_beside = move(after(across, *gates), 1, 0)
        return [x, move(x, 1, 0), across, across_beside]

    def pinned(x, space=pltpu.HBM):
        return pltpu.with_memory_space_constraint(x, space)

    routes_t = routes.T
    block = pl.pallas_call(
        pack_kernel,
        out_shape=pltpu.VMEM((tokens, LANES + width), grad_out.dtype),
        in_specs=[hbm] * 3,
        out_specs=vmem,
        scratch_shapes=[
            pltpu.VMEM(routes_t.shape, routes.dtype),
            pltpu.VMEM(routes_t.shape, combine.dtype),
            pltpu.SemaphoreType.DMA((3,)),
        ],
        compiler_params=params,
    )(pinned(grad_out), pinned(routes_t), pinned(combine.T))
    weights, cache = pl.pallas_call(
        load_kernel,
        out_shape=[
            pltpu.VMEM((hidden, width), down_weight.dtype),
            pltpu.VMEM((slots, hidden), hidden_cache.dtype),
        ],
        in_specs=[hbm] * 2,
        out_specs=[vmem] * 2,
        scratch_shapes=[pltpu.SemaphoreType.DMA((2,))],
        compiler_params=params,
        cost_estimate=free,
    )(pinned(down_weight[0]), pinned(hidden_cache[0]))

    early, late = (3, 1, 0), 2
    order = (*[j for j in early if j], late)
    groups = [[(i, j) for i in range(nodes)] for j in (*early, late)]
    far = {j: move(block, 0, j) for j in (2, 3, 1)}
    blocks = []
    for j in early:
        blocks += over_nodes(far[j] if j else block, cache)
    rows = len(blocks) * capacity
    picked, chosen, scales = pl.pallas_call(
        functools.partial(pick_kernel, groups[:-1]),
        out_shape=[
            pltpu.VMEM((slots, width), jnp.bfloat16),
            pltpu.VMEM((rows, LANES), jnp.float32),
            pltpu.VMEM((rows, LANES), jnp.float32),
        ],
        in_specs=[vmem] * len(blocks),
        out_specs=[vmem] * 3,
        compiler_params=params,
        cost_estimate=pl.CostEstimate(
            flops=2 * rows * nodes * tokens * width, bytes_accessed=1 << 22, transcendentals=0
        ),
    )(*blocks)
    blocks = over_nodes(far[late])
    held = [chosen, scales, weights, cache, picked]
    all_rows, *terms = pl.pallas_call(
        functools.partial(expert_kernel, groups),
        out_shape=[jax.ShapeDtypeStruct((slots, hidden), jnp.bfloat16)]
        + [jax.ShapeDtypeStruct((1, nodes * tokens), jnp.float32)] * LINE
        + [pltpu.VMEM(picked.shape, picked.dtype)],
        in_specs=[vmem] * (nodes + len(held)),
        out_specs=[vmem] * (2 + LINE),
        input_output_aliases={len(held) - 1: 1 + LINE},
        compiler_params=params,
        cost_estimate=free,
    )(*[pinned(x, pltpu.VMEM) for x in held], *blocks)
    terms = dict(zip((*early, late), terms))
    d_hidden = pl.pallas_call(
        functools.partial(place_kernel, groups),
        out_shape=jax.ShapeDtypeStruct((slots, hidden), jnp.bfloat16),
        in_specs=[vmem],
        out_specs=vmem,
        compiler_params=params,
        cost_estimate=free,
    )(all_rows)

    back = [move(terms[j], 0, j) if j else terms[j] for j in (0, *order)]
    back = jnp.concatenate(back, axis=0)
    back, routes_t, node, local = lax.optimization_barrier((back, routes_t, node, local))
    back = after(back, d_hidden)
    d_combine_t = jnp.zeros(routes_t.shape, jnp.float32)
    for i in range(nodes):
        returned = (move(back, i, 0) if i else back)[:, i * tokens : (i + 1) * tokens]
        for g, j in enumerate((0, *order)):
            expert = (node ^ i) * LINE + (local ^ j)
            d_combine_t += jnp.where(routes_t == expert, returned[g], jnp.float32(0))
    return d_hidden[None], d_combine_t.T


def per_device(grad_out, routes, combine, hidden_cache, down_weight):
    nodes = lax.axis_size("node")
    locals_ = lax.axis_size("local")
    tokens, top = routes.shape
    fits = nodes * tokens == LANES and tokens == 4 * top and hidden_cache.shape[1] == 8 * tokens
    if nodes == TOPNODES == 4 and locals_ == LINE and fits:
        return exchanged(grad_out, routes, combine, hidden_cache, down_weight)
    return routed(grad_out, routes, combine, hidden_cache, down_weight)


def solution(mesh):
    placed = (
        P(("rep", "node", "local"), None),
        P(("rep", "node", "local"), None),
        P(("rep", "node", "local"), None),
        P(("rep", "node", "local"), None, None),
        P(("node", "local"), None, None),
    )
    return jax.shard_map(
        per_device,
        mesh=mesh,
        in_specs=placed,
        out_specs=(P(("rep", "node", "local"), None, None), P(("rep", "node", "local"), None)),
        check_vma=False,
    )
```

```python
import functools

import jax
import jax.numpy as jnp
from jax import lax
from jax.experimental import pallas as pl
from jax.experimental.pallas import tpu as pltpu
from jax.sharding import PartitionSpec as P

TOPNODES = 4


def slot_tables(routes, combine, experts_all, capacity):
    onehot = (routes[:, :, None] == lax.iota(jnp.int32, experts_all)[None, None, :]).astype(
        jnp.float32
    )
    hit_mask = jnp.sum(onehot, axis=1)
    weight_te = jnp.einsum("tke,tk->te", onehot, combine.astype(jnp.float32))
    slot_rank = jnp.cumsum(hit_mask, axis=0) - hit_mask
    select = hit_mask[:, :, None] * (
        slot_rank[:, :, None] == lax.iota(jnp.float32, capacity)[None, None, :]
    ).astype(jnp.float32)
    return (onehot, hit_mask, select, select * weight_te[:, :, None])


def routed(grad_out, routes, combine, hidden_cache, down_weight):
    node_count = lax.axis_size("node")
    local_count = lax.axis_size("local")
    experts_all = node_count * local_count
    slots_all = hidden_cache.shape[1]
    capacity = slots_all // experts_all
    tok_rows = grad_out.shape[0]
    width = grad_out.shape[1]
    onehot, hit_mask, select, scaled = slot_tables(routes, combine, experts_all, capacity)
    per_node = tok_rows * TOPNODES // node_count
    node_hit = jnp.max(hit_mask.reshape(tok_rows, node_count, local_count), axis=2)
    node_rank = jnp.cumsum(node_hit, axis=0) - node_hit
    placement = node_hit[:, :, None] * (
        node_rank[:, :, None] == lax.iota(jnp.float32, per_node)[None, None, :]
    ).astype(jnp.float32)
    node_rows = jnp.einsum(
        "tnm,td->nmd", placement.astype(jnp.bfloat16), grad_out, preferred_element_type=jnp.float32
    ).astype(jnp.bfloat16)
    weight_table = jnp.einsum(
        "tnm,tnq->nmq", placement, scaled.reshape(tok_rows, node_count, local_count * capacity)
    ).astype(jnp.bfloat16)
    node_rows, weight_table = (
        lax.all_to_all(node_rows, "node", split_axis=0, concat_axis=0, tiled=True),
        lax.all_to_all(weight_table, "node", split_axis=0, concat_axis=0, tiled=True),
    )
    fan_mask = (weight_table != 0).astype(jnp.bfloat16)
    row_block = jnp.einsum(
        "nmq,nmd->nqd", fan_mask, node_rows, preferred_element_type=jnp.float32
    ).astype(jnp.bfloat16)
    weights = jnp.sum(weight_table.astype(jnp.float32), axis=1).astype(jnp.bfloat16)
    row_block = row_block.reshape(node_count, local_count, capacity, width)
    weights = weights.reshape(node_count, local_count, capacity)
    row_block, weights = (
        lax.all_to_all(row_block, "local", split_axis=1, concat_axis=1, tiled=True),
        lax.all_to_all(weights, "local", split_axis=1, concat_axis=1, tiled=True),
    )
    flat_rows = row_block.reshape(slots_all, width)
    products = lax.dot_general(
        flat_rows, down_weight[0], (((1,), (1,)), ((), ())), preferred_element_type=jnp.float32
    )
    d_hidden = (weights.reshape(slots_all, 1).astype(jnp.float32) * products).astype(jnp.bfloat16)[
        None
    ]
    slot_terms = jnp.sum(products * hidden_cache[0].astype(jnp.float32), axis=1)
    slot_terms = slot_terms.reshape(node_count, local_count, capacity)
    returned = lax.all_to_all(
        lax.all_to_all(slot_terms, "node", split_axis=0, concat_axis=0, tiled=True),
        "local",
        split_axis=1,
        concat_axis=1,
        tiled=True,
    )
    returned = returned.reshape(experts_all, capacity)
    per_expert = jnp.einsum("tec,ec->te", select, returned)
    d_combine = jnp.einsum("tke,te->tk", onehot, per_expert)
    return (d_hidden, d_combine)


LANES = 128
LINE = 4
PARTS = 4
WORK_BYTES = 16 * 1024 * 1024
CHUNK = 512


def pack_kernel(rows_hbm, routes_hbm, combine_hbm, block_ref, routes_ref, combine_ref, sems):
    copies = [
        pltpu.make_async_copy(routes_hbm, routes_ref, sems.at[0]),
        pltpu.make_async_copy(combine_hbm, combine_ref, sems.at[1]),
    ]
    quarter = rows_hbm.shape[1] // PARTS
    for p in range(PARTS):
        part = rows_hbm.at[:, p * quarter : (p + 1) * quarter]
        place = block_ref.at[:, LANES + p * quarter : LANES + (p + 1) * quarter]
        copies.append(pltpu.make_async_copy(part, place, sems.at[2 + p]))
    for copy in copies:
        copy.start()
    for copy in copies[:2]:
        copy.wait()
    top, tokens = routes_ref.shape
    table = jnp.concatenate(
        [routes_ref[...].astype(jnp.float32), combine_ref[...].astype(jnp.float32)], axis=0
    )
    table = jnp.concatenate([table] * (LANES // tokens), axis=1)
    fill = jnp.zeros((block_ref.shape[0] - 2 * top, LANES), jnp.float32)
    block_ref[:, :LANES] = jnp.concatenate([table, fill], axis=0).astype(block_ref.dtype)
    for copy in copies[2:]:
        copy.wait()


def load_kernel(weight_hbm, cache_hbm, weight_ref, cache_ref, sems):
    copies = [
        pltpu.make_async_copy(weight_hbm, weight_ref, sems.at[0]),
        pltpu.make_async_copy(cache_hbm, cache_ref, sems.at[1]),
    ]
    for copy in copies:
        copy.start()
    for copy in copies:
        copy.wait()


def pick_rows(blocks, expert, capacity, picked, at):
    tokens = blocks[0].shape[0]
    top = tokens // 4
    span = len(blocks) * tokens
    rows = len(blocks) * capacity
    owner = lax.broadcasted_iota(jnp.int32, (1, span), 1) // tokens
    earlier = lax.broadcasted_iota(jnp.int32, (span, span), 0)
    later = lax.broadcasted_iota(jnp.int32, (span, span), 1)
    before = ((earlier < later) & (earlier // tokens == later // tokens)).astype(jnp.bfloat16)
    table = jnp.zeros((2 * top, span), jnp.float32)
    for i, block in enumerate(blocks):
        table = jnp.where(owner == i, block[: 2 * top, :LANES].astype(jnp.float32)[:, :span], table)
    match = (table[:top] == expert).astype(jnp.float32)
    hit = jnp.sum(match, axis=0, keepdims=True)
    weight = jnp.sum(match * table[top:], axis=0, keepdims=True)
    rank = jnp.dot(
        jnp.broadcast_to(hit, (top, span)).astype(jnp.bfloat16),
        before,
        preferred_element_type=jnp.float32,
    )[:1]
    target = rank + (owner * capacity).astype(jnp.float32)
    slot_of = lax.broadcasted_iota(jnp.int32, (rows, span), 0).astype(jnp.float32)
    choose = jnp.where((slot_of == target) & (hit > 0), jnp.float32(1), jnp.float32(0))
    source_rows = jnp.concatenate([block[:, LANES:] for block in blocks], axis=0)
    picked[at : at + rows, :] = jnp.dot(
        choose.astype(jnp.bfloat16), source_rows, preferred_element_type=jnp.float32
    ).astype(jnp.bfloat16)
    return choose, jnp.sum(choose * weight, axis=1, keepdims=True)


def source_start(source, capacity):
    i, j = source
    index = (lax.axis_index("node") ^ i) * LINE + (lax.axis_index("local") ^ j)
    return pl.multiple_of(index * capacity, capacity)


def pick_kernel(groups, *refs):
    *blocks, picked, chosen_ref, scale_ref = refs
    expert = (lax.axis_index("node") * LINE + lax.axis_index("local")).astype(jnp.float32)
    capacity = blocks[0].shape[0] // 2
    at = 0
    for g, group in enumerate(groups):
        mine = blocks[g * len(group) : (g + 1) * len(group)]
        choose, scale = pick_rows(mine, expert, capacity, picked, at)
        rows = choose.shape[0]
        chosen_ref[at : at + rows, :] = choose
        scale_ref[at : at + rows, :] = jnp.broadcast_to(scale, (rows, LANES))
        at += rows


def expert_kernel(groups, *refs):
    members = len(groups[-1])
    chosen_ref, scale_ref, weights, cache, _ = refs[:5]
    blocks, rows_ref = refs[5 : 5 + members], refs[5 + members]
    term_refs, picked = refs[6 + members : -1], refs[-1]
    hidden = weights.shape[0]
    capacity = blocks[0].shape[0] // 2
    expert = (lax.axis_index("node") * LINE + lax.axis_index("local")).astype(jnp.float32)
    early = chosen_ref.shape[0]
    choose, scale = pick_rows(blocks, expert, capacity, picked, early)
    scale = jnp.concatenate([scale_ref[:, :1], scale], axis=0)
    choose = jnp.concatenate([chosen_ref[...], choose], axis=0)
    places = [source_start(source, capacity) for group in groups for source in group]
    terms = jnp.zeros((len(places) * capacity, 1), jnp.float32)
    for c in range(0, hidden, CHUNK):
        part = slice(c, c + CHUNK)
        products = lax.dot_general(
            picked[...], weights[part, :], (((1,), (1,)), ((), ())), preferred_element_type=jnp.float32
        )
        kept = [cache[pl.ds(place, capacity), part] for place in places]
        kept = jnp.concatenate(kept, axis=0).astype(jnp.float32)
        terms = terms + jnp.sum(products * kept, axis=1, keepdims=True)
        rows_ref[:, part] = (scale * products).astype(rows_ref.dtype)
    spread = choose * terms
    rows = members * capacity
    for g, term_ref in enumerate(term_refs):
        term_ref[...] = jnp.sum(spread[g * rows : (g + 1) * rows], axis=0, keepdims=True)


def place_kernel(groups, rows_ref, out_ref):
    sources = [source for group in groups for source in group]
    capacity = out_ref.shape[0] // len(sources)
    for s, source in enumerate(sources):
        out_ref[pl.ds(source_start(source, capacity), capacity), :] = rows_ref[
            s * capacity : (s + 1) * capacity, :
        ]


def exchanged(grad_out, routes, combine, hidden_cache, down_weight):
    nodes = lax.axis_size("node")
    node = lax.axis_index("node")
    local = lax.axis_index("local")
    tokens, width = grad_out.shape
    hidden = down_weight.shape[1]
    slots = hidden_cache.shape[1]
    capacity = slots // (nodes * LINE)
    vmem = pl.BlockSpec(memory_space=pltpu.VMEM)
    hbm = pl.BlockSpec(memory_space=pltpu.HBM)
    params = pltpu.CompilerParams(vmem_limit_bytes=WORK_BYTES)
    free = pl.CostEstimate(flops=1, bytes_accessed=1, transcendentals=0)

    def move(x, node_mask, local_mask):
        pairs = [
            (n * LINE + l, (n ^ node_mask) * LINE + (l ^ local_mask))
            for n in range(nodes)
            for l in range(LINE)
        ]
        return lax.ppermute(x, ("node", "local"), pairs)

    def after(x, *others):
        return lax.optimization_barrier((x, *others))[0]

    def over_nodes(x, *gates):
        across = move(x, 2, 0)
        across_beside = move(after(across, *gates), 1, 0)
        return [x, move(x, 1, 0), across, across_beside]

    def pinned(x, space=pltpu.HBM):
        return pltpu.with_memory_space_constraint(x, space)

    routes_t = routes.T
    block = pl.pallas_call(
        pack_kernel,
        out_shape=pltpu.VMEM((tokens, LANES + width), grad_out.dtype),
        in_specs=[hbm] * 3,
        out_specs=vmem,
        scratch_shapes=[
            pltpu.VMEM(routes_t.shape, routes.dtype),
            pltpu.VMEM(routes_t.shape, combine.dtype),
            pltpu.SemaphoreType.DMA((2 + PARTS,)),
        ],
        compiler_params=params,
    )(pinned(grad_out), pinned(routes_t), pinned(combine.T))
    weights, cache = pl.pallas_call(
        load_kernel,
        out_shape=[
            pltpu.VMEM((hidden, width), down_weight.dtype),
            pltpu.VMEM((slots, hidden), hidden_cache.dtype),
        ],
        in_specs=[hbm] * 2,
        out_specs=[vmem] * 2,
        scratch_shapes=[pltpu.SemaphoreType.DMA((2,))],
        compiler_params=params,
        cost_estimate=free,
    )(pinned(down_weight[0]), pinned(hidden_cache[0]))

    early, late = (3, 1, 0), 2
    order = (*[j for j in early if j], late)
    groups = [[(i, j) for i in range(nodes)] for j in (*early, late)]
    far = {j: move(block, 0, j) for j in (2, 3, 1)}
    blocks = []
    for j in early:
        blocks += over_nodes(far[j] if j else block, cache)
    rows = len(blocks) * capacity
    picked, chosen, scales = pl.pallas_call(
        functools.partial(pick_kernel, groups[:-1]),
        out_shape=[
            pltpu.VMEM((slots, width), jnp.bfloat16),
            pltpu.VMEM((rows, LANES), jnp.float32),
            pltpu.VMEM((rows, LANES), jnp.float32),
        ],
        in_specs=[vmem] * len(blocks),
        out_specs=[vmem] * 3,
        compiler_params=params,
        cost_estimate=pl.CostEstimate(
            flops=2 * rows * nodes * tokens * width, bytes_accessed=1 << 22, transcendentals=0
        ),
    )(*blocks)
    blocks = over_nodes(far[late])
    held = [chosen, scales, weights, cache, picked]
    all_rows, *terms = pl.pallas_call(
        functools.partial(expert_kernel, groups),
        out_shape=[jax.ShapeDtypeStruct((slots, hidden), jnp.bfloat16)]
        + [jax.ShapeDtypeStruct((1, nodes * tokens), jnp.float32)] * LINE
        + [pltpu.VMEM(picked.shape, picked.dtype)],
        in_specs=[vmem] * (nodes + len(held)),
        out_specs=[vmem] * (2 + LINE),
        input_output_aliases={len(held) - 1: 1 + LINE},
        compiler_params=params,
        cost_estimate=free,
    )(*[pinned(x, pltpu.VMEM) for x in held], *blocks)
    terms = dict(zip((*early, late), terms))
    d_hidden = pl.pallas_call(
        functools.partial(place_kernel, groups),
        out_shape=jax.ShapeDtypeStruct((slots, hidden), jnp.bfloat16),
        in_specs=[vmem],
        out_specs=vmem,
        compiler_params=params,
        cost_estimate=free,
    )(all_rows)

    back = [move(terms[j], 0, j) if j else terms[j] for j in (0, *order)]
    back = jnp.concatenate(back, axis=0)
    back, routes_t, node, local = lax.optimization_barrier((back, routes_t, node, local))
    back = after(back, d_hidden)
    d_combine_t = jnp.zeros(routes_t.shape, jnp.float32)
    for i in range(nodes):
        returned = (move(back, i, 0) if i else back)[:, i * tokens : (i + 1) * tokens]
        for g, j in enumerate((0, *order)):
            expert = (node ^ i) * LINE + (local ^ j)
            d_combine_t += jnp.where(routes_t == expert, returned[g], jnp.float32(0))
    return d_hidden[None], d_combine_t.T


def per_device(grad_out, routes, combine, hidden_cache, down_weight):
    nodes = lax.axis_size("node")
    locals_ = lax.axis_size("local")
    tokens, top = routes.shape
    fits = nodes * tokens == LANES and tokens == 4 * top and hidden_cache.shape[1] == 8 * tokens
    if nodes == TOPNODES == 4 and locals_ == LINE and fits:
        return exchanged(grad_out, routes, combine, hidden_cache, down_weight)
    return routed(grad_out, routes, combine, hidden_cache, down_weight)


def solution(mesh):
    placed = (
        P(("rep", "node", "local"), None),
        P(("rep", "node", "local"), None),
        P(("rep", "node", "local"), None),
        P(("rep", "node", "local"), None, None),
        P(("node", "local"), None, None),
    )
    return jax.shard_map(
        per_device,
        mesh=mesh,
        in_specs=placed,
        out_specs=(P(("rep", "node", "local"), None, None), P(("rep", "node", "local"), None)),
        check_vma=False,
    )
```
